32 devices in a mesh: grp: 2 (over y), dp: 16 (over z, x, core).
Axes of the slice: x: 2, y: 2, z: 4, core: 2. Of those that a mesh axis runs over, the one named last changes fastest.
Arguments:
- acts: bfloat16 [16384, 2560], P(('grp', 'dp')), may hold values from -18 to 18
- cotangents: bfloat16 [16384, 768], P(('grp', 'dp')), may hold values from -6 to 6
Outputs:
- update: float32 [2560, 768], P(('grp', 'dp'))
The draws below stay inside these ranges and needn't reach their ends.
All inputs are finite; a program needn't handle non-finite values. Where the reference program divides by a largest or mean magnitude, that divisor is 1e-20 or more.
Results may differ from the reference program's by a relative error of at most 0.013.
Values may be sent and summed in bfloat16 or wider, within the bound.
A program may use at most 64 MiB of HBM per device.

```python
import jax
import jax.numpy as jnp
from jax import lax

D = 2560
R = 768
BLK = 128
ITERS = 8
TOK_DEV = 512
TOKENS = 16384
NA = 20
NG = 6


def draw_acts(key, part):
    key_vals = jax.random.fold_in(key, 11)
    key_perm = jax.random.fold_in(key, 23)
    devcount = TOKENS // TOK_DEV
    span = D // devcount
    values = jnp.clip(jax.random.normal(key_vals, (TOKENS, D), jnp.float32), -6.0, 6.0)
    slope = 0.5
    column = jnp.arange(D, dtype=jnp.float32)
    col_scale = jnp.power(10.0, -slope * column / D)
    paired = jax.random.permutation(key_perm, devcount)
    row_dev = jnp.arange(TOKENS, dtype=jnp.int32) // TOK_DEV
    col_block = jnp.arange(D, dtype=jnp.int32) // span
    spike = jnp.where(paired[row_dev][:, None] == col_block[None, :], 3.0, 1.0)
    return (values * spike * col_scale[None, :]).astype(jnp.bfloat16)


def level_of(key, shape, split, low, largest):
    level, own = 1.0, jax.random.fold_in(key, 6)
    for dim, parts in split:
        draws = jnp.exp(jax.random.uniform(jax.random.fold_in(own, dim), (parts,), jnp.float32, low / len(split), largest / len(split)))
        level = level * jnp.repeat(draws, shape[dim] // parts).reshape([-1 if axis == dim else 1 for axis in range(len(shape))])
    return level


def normal_values(stream_key, dims, scale, reach, cuts=(), kind=jnp.bfloat16):
    result = jax.random.normal(stream_key, dims, jnp.float32) * scale
    if len(cuts) > 0:
        result = level_of(stream_key, dims, cuts, -0.22, 0.18) * result
    return jnp.clip(result, min=-reach, max=reach).astype(kind)


def setup_inputs(seed: int = 0) -> dict:
    streams_of = jax.random.split(jax.random.key(seed), 3)
    return {
        "acts": draw_acts(jax.random.fold_in(streams_of[2], 71), 0),
        "cotangents": normal_values(streams_of[1], (TOKENS, R), 1.0, 6.0, ((0, 32),)),
    }


def newton_inverse(blocks):
    eye = jnp.eye(BLK, dtype=jnp.float32)
    trace = lax.optimization_barrier(jnp.sum(blocks * eye, axis=(1, 2)))
    damped = blocks + (0.1 * (trace / BLK + 1e-06))[:, None, None] * eye
    scale = 1.0 / lax.optimization_barrier(jnp.max(lax.optimization_barrier(jnp.sum(jnp.abs(damped), axis=2)), axis=1))
    approx = scale[:, None, None] * eye
    for step in range(ITERS):
        product = jnp.einsum('nij,njk->nik', damped, approx, precision=lax.Precision.HIGHEST)
        approx = jnp.einsum('nij,njk->nik', approx, 2.0 * eye - product, precision=lax.Precision.HIGHEST)
    return approx

def reference(acts, cotangents):
    tokens = acts.shape[0]
    x_blocks = acts.astype(jnp.float32).reshape(tokens, NA, BLK)
    d_blocks = cotangents.astype(jnp.float32).reshape(tokens, NG, BLK)
    fa = jnp.einsum('tbi,tbj->bij', x_blocks, x_blocks, precision=lax.Precision.HIGHEST) / TOKENS
    fg = jnp.einsum('tbi,tbj->bij', d_blocks, d_blocks, precision=lax.Precision.HIGHEST) / TOKENS
    inverse16 = newton_inverse(jnp.concatenate([fa, fg], axis=0)).astype(jnp.bfloat16).astype(jnp.float32)
    xpre = jnp.einsum('tbi,bij->tbj', x_blocks, inverse16[:NA], precision=lax.Precision.HIGHEST)
    xpre = xpre.astype(jnp.bfloat16).reshape(tokens, D)
    left = jnp.dot(xpre.T, cotangents, preferred_element_type=jnp.float32) / TOKENS
    natural = jnp.einsum('rci,cij->rcj', left.reshape(D, NG, BLK), inverse16[NA:], precision=lax.Precision.HIGHEST).reshape(D, R)
    quad = jnp.mean(natural * natural)
    return natural / jnp.sqrt(quad + 1e-06)
```

```python
import functools

import jax
import jax.numpy as jnp
from jax import lax
from jax.experimental import pallas as pl
from jax.experimental.pallas import tpu as pltpu
from jax.sharding import PartitionSpec as P

D = 2560
R = 768
BLK = 128
ITERS = 8
NA = D // BLK
NG = R // BLK
QROWS = D // 4
QBLK = QROWS // BLK
HALF = QROWS // 2
CCOLS = R // 2
CBLK = CCOLS // BLK
SLOTS = 4
MESH = pl.DeviceIdType.MESH
F32 = jnp.float32
BF16 = jnp.bfloat16


def dot(a, b):
    return jnp.dot(a, b, preferred_element_type=F32)


def dot_t(a, b):
    return lax.dot_general(a, b, (((0,), (0,)), ((), ())), preferred_element_type=F32)


def split(a):
    hi = a.astype(BF16)
    return hi, (a - hi.astype(F32)).astype(BF16)


def dot3(a, b):
    ah, al = split(a)
    bh, bl = split(b)
    return dot(jnp.concatenate([ah, ah, al], axis=1), jnp.concatenate([bh, bl, bh], axis=0))


def kernel(
    groups, width, total, rows,
    x_ref, g_ref, out_ref,
    xt, fpart, f1recv, f2send, f2recv, f3send, f3recv,
    m1send, m1recv, macc, m2a, m2s, m2b, mq,
    inv_own, inv_a, inv_g, nat, fin_send, fin_recv, qsend, qrecv,
    f1_ss, f1_rs, f2_ss, f2_rs, f3_ss, f3_rs, m1_ss, m1_rs, ma_ss, ma_rs,
    mb_ss, mb_rs, inv_ss, inv_rs, fin_ss, fin_rs, q_ss, q_rs,
):
    devices = groups * width
    rest_n = devices // 8
    owners = devices // 4
    dp_rest = width // 4
    gi = lax.axis_index("grp")
    di = lax.axis_index("dp")
    me = gi * width + di
    core = lax.rem(di, 2)
    x = lax.rem(lax.div(di, 2), 2)
    y = lax.rem(gi, 2)
    q = 2 * y + x
    rest = lax.div(gi, 2) * dp_rest + lax.div(di, 4)

    def at(yy, xx, zz, cc):
        return (
            lax.div(zz, dp_rest) * 2 + yy,
            lax.rem(zz, dp_rest) * 4 + xx * 2 + cc,
        )

    def linear(d):
        return (lax.div(d, width), lax.rem(d, width))

    def rcopy(src, dst, ss, rs, dev):
        return pltpu.make_async_remote_copy(
            src_ref=src, dst_ref=dst, send_sem=ss, recv_sem=rs,
            device_id=dev, device_id_type=MESH,
        )

    barrier = pltpu.get_barrier_semaphore()

    @pl.loop(0, devices)
    def _(d):
        @pl.when(d != me)
        def _():
            pl.semaphore_signal(barrier, inc=1, device_id=linear(d), device_id_type=MESH)

    zero = jnp.zeros((BLK, BLK), BF16)

    @pl.loop(0, 4)
    def _(qq):
        for t in range(QBLK):
            b = qq * QBLK + t
            xb = x_ref[:, pl.ds(pl.multiple_of(b * BLK, BLK), BLK)]
            xbt = xb.T
            xt[b] = xbt
            fpart[t % 2, qq, t // 2] = dot(xbt, xb).astype(BF16)
        fpart[0, qq, 3] = zero
        fpart[1, qq, 3] = zero

    for c in range(NG):
        gb = g_ref[:, c * BLK:(c + 1) * BLK]
        fg = dot_t(gb, gb).astype(BF16)
        if c < 4:
            fpart[1, c, 2] = fg
        else:
            fpart[0, c - 4, 3] = fg

    pl.semaphore_wait(barrier, devices - 1)
    other = at(y, x, rest, 1 - core)
    f1 = rcopy(fpart.at[1 - core], f1recv, f1_ss.at[0], f1_rs.at[0], other)
    f1.start()

    g_other = g_ref[:, pl.ds(pl.multiple_of((1 - core) * CCOLS, BLK), CCOLS)]

    def m1_copy(qq):
        return rcopy(m1send.at[qq], m1recv.at[qq], m1_ss.at[qq], m1_rs.at[qq], other)

    @pl.loop(0, 4)
    def _(qq):
        for t in range(QBLK):
            m1send[qq, t * BLK:(t + 1) * BLK, :] = dot(xt[qq * QBLK + t], g_other).astype(BF16)
        m1_copy(qq).start()

    f1.wait_recv()

    def f1_sum(qq, s):
        return fpart[core, qq, s].astype(F32) + f1recv[qq, s].astype(F32)

    chips = [(y, 1 - x), (1 - y, x), (1 - y, 1 - x)]
    f2 = []
    for k, (yy, xx) in enumerate(chips):
        qq = 2 * yy + xx
        for s in range(SLOTS):
            f2send[k, s] = f1_sum(qq, s).astype(BF16)
        c2 = rcopy(f2send.at[k], f2recv.at[k], f2_ss.at[k], f2_rs.at[k], at(yy, xx, rest, core))
        c2.start()
        f2.append(c2)

    g_mine = g_ref[:, pl.ds(pl.multiple_of(core * CCOLS, BLK), CCOLS)]

    @pl.loop(0, 4)
    def _(qq):
        m1_copy(qq).wait_recv()
        for t in range(QBLK):
            part = dot(xt[qq * QBLK + t], g_mine)
            sl = slice(t * BLK, (t + 1) * BLK)
            macc[qq, sl, :] = (part + m1recv[qq, sl, :].astype(F32)).astype(BF16)

    at_x = at(y, 1 - x, rest, core)
    at_y = at(1 - y, x, rest, core)
    ma = []
    for i in range(2):
        for h in range(2):
            k = 2 * h + i
            quarter = 2 * i + (1 - x) if h == 0 else 2 * (1 - y) + i
            ca = rcopy(
                macc.at[quarter, pl.ds(h * HALF, HALF)], m2a.at[k],
                ma_ss.at[k], ma_rs.at[k], at_x if h == 0 else at_y,
            )
            ca.start()
            ma.append(ca)

    for c2 in f2:
        c2.wait_recv()
    for s in range(SLOTS):
        f = f1_sum(q, s)
        for k in range(3):
            f = f + f2recv[k, s].astype(F32)
        f3send[s] = f.astype(BF16)

    def f3_copy(s, src):
        return rcopy(f3send.at[s], f3recv.at[src], f3_ss.at[s], f3_rs.at[src], at(y, x, s, core))

    for s in range(SLOTS):
        @pl.when(rest != s)
        def _():
            f3_copy(s, rest).start()

    f3recv[rest] = f3send[lax.rem(rest, SLOTS)]

    @pl.when(rest < SLOTS)
    def _():
        @pl.loop(0, rest_n)
        def _(z):
            @pl.when(z != rest)
            def _():
                f3_copy(0, z).wait_recv()

    if rest_n > SLOTS:
        @pl.when(rest >= SLOTS)
        def _():
            @pl.loop(0, rest_n)
            def _(z):
                f3recv[z] = zero

    factor = f3recv[0].astype(F32)
    for z in range(1, rest_n):
        factor = factor + f3recv[z].astype(F32)
    factor = factor * (1.0 / total)

    eye = (
        lax.broadcasted_iota(jnp.int32, (BLK, BLK), 0)
        == lax.broadcasted_iota(jnp.int32, (BLK, BLK), 1)
    ).astype(F32)
    trace = jnp.sum(jnp.sum(factor * eye, axis=1, keepdims=True), axis=0, keepdims=True)
    damped = factor + (0.1 * (trace / BLK + 1e-06)) * eye
    peak = jnp.max(jnp.sum(jnp.abs(damped), axis=1, keepdims=True), axis=0, keepdims=True)
    scale = 1.0 / peak
    approx = scale * (2.0 * eye - scale * damped)
    for _ in range(ITERS - 5):
        approx = dot3(approx, 2.0 * eye - dot3(damped, approx))

    for ca in ma:
        ca.wait_recv()
    for i in range(2):
        for h in range(2):
            k = 2 * h + i
            quarter = 2 * i + x if h == 0 else 2 * y + i
            m2s[k] = (
                macc[quarter, h * HALF:(h + 1) * HALF, :].astype(F32) + m2a[k].astype(F32)
            ).astype(BF16)
    mb = [
        rcopy(m2s.at[1 - y], m2b.at[0], mb_ss.at[0], mb_rs.at[0], at_y),
        rcopy(m2s.at[2 + 1 - x], m2b.at[1], mb_ss.at[1], mb_rs.at[1], at_x),
    ]
    for cb in mb:
        cb.start()

    for _ in range(4):
        approx = dot3(approx, 2.0 * eye - dot3(damped, approx))
    inv_own[...] = approx.astype(BF16)

    slot = 2 * rest + core
    is_a = slot < QBLK
    is_g = jnp.logical_or(slot == QBLK, jnp.logical_and(slot == QBLK + 1, q < NG - 4))
    gidx = (slot - QBLK) * 4 + q
    ghalf = lax.div(gidx, CBLK)

    def a_copy(i, t):
        return rcopy(
            inv_own, inv_a.at[t], inv_ss.at[i], inv_rs.at[t],
            at(y, x, lax.div(i, 2), lax.rem(i, 2)),
        )

    def g_dev(i):
        chip = lax.div(i, rest_n)
        return at(lax.div(chip, 2), lax.rem(chip, 2), lax.rem(i, rest_n), ghalf)

    def g_copy(i, c):
        return rcopy(inv_own, inv_g.at[c], inv_ss.at[i], inv_rs.at[QBLK + c], g_dev(i))

    def not_me(i):
        gg, dd = g_dev(i)
        return gg * width + dd != me

    @pl.when(is_a)
    def _():
        @pl.loop(0, owners)
        def _(i):
            @pl.when(i != slot)
            def _():
                a_copy(i, slot).start()
        inv_a[slot] = inv_own[...]

    @pl.when(is_g)
    def _():
        @pl.loop(0, 4 * rest_n)
        def _(i):
            @pl.when(not_me(i))
            def _():
                g_copy(i, lax.rem(gidx, CBLK)).start()

        @pl.when(ghalf == core)
        def _():
            inv_g[lax.rem(gidx, CBLK)] = inv_own[...]

    for cb in mb:
        cb.wait_recv()
    for h in range(2):
        kept = m2s[y] if h == 0 else m2s[2 + x]
        mq[h * HALF:(h + 1) * HALF, :] = (
            (kept.astype(F32) + m2b[h].astype(F32)) * (1.0 / total)
        ).astype(BF16)

    for c in range(CBLK):
        @pl.when(jnp.logical_not(jnp.logical_and(is_g, gidx == core * CBLK + c)))
        def _():
            g_copy(0, c).wait_recv()
    for t in range(QBLK):
        @pl.when(slot != t)
        def _():
            a_copy(0, t).wait_recv()

    for t in range(QBLK):
        left = dot_t(inv_a[t], mq[t * BLK:(t + 1) * BLK, :])
        for c in range(CBLK):
            hi, lo = split(left[:, c * BLK:(c + 1) * BLK])
            ginv = inv_g[c]
            nat[t * BLK:(t + 1) * BLK, c * BLK:(c + 1) * BLK] = dot(hi, ginv) + dot(lo, ginv)

    def fin_copy(k, r):
        return rcopy(
            fin_send.at[k], fin_recv.at[r], fin_ss.at[k], fin_rs.at[r], linear(q * owners + k)
        )

    if rows % 16:
        fin_send[...] = jnp.zeros_like(fin_send)
    for k in range(owners):
        fin_send[k, :rows, :] = nat[k * rows:(k + 1) * rows, :].astype(BF16)

        @pl.when(q * owners + k != me)
        def _():
            fin_copy(k, slot).start()

        @pl.when(q * owners + k == me)
        def _():
            fin_recv[slot] = fin_send[k]

    from_me = lax.div(me, owners) == q

    @pl.loop(0, owners)
    def _(r):
        @pl.when(jnp.logical_not(jnp.logical_and(from_me, r == slot)))
        def _():
            fin_copy(0, r).wait_recv()

    square = jnp.zeros((1, 1), F32)
    natural = []
    for c in range(2):
        part = fin_recv[c].astype(F32)
        for z in range(1, rest_n):
            part = part + fin_recv[2 * z + c].astype(F32)
        part = part[:rows, :]
        natural.append(part)
        square = square + jnp.sum(
            jnp.sum(part * part, axis=0, keepdims=True), axis=1, keepdims=True
        )
    qsend[...] = jnp.broadcast_to(square, qsend.shape)
    qrecv[me] = qsend[...]

    def q_copy(d, src):
        return rcopy(qsend, qrecv.at[src], q_ss.at[d], q_rs.at[src], linear(d))

    @pl.loop(0, devices)
    def _(d):
        @pl.when(d != me)
        def _():
            q_copy(d, me).start()

    @pl.loop(0, devices)
    def _(d):
        @pl.when(d != me)
        def _():
            q_copy(0, d).wait_recv()

    quad = jnp.sum(qrecv[...], axis=0)[:1, :1] / (D * R)
    factor_out = lax.rsqrt(quad + 1e-06)
    for c in range(2):
        out_ref[:, c * CCOLS:(c + 1) * CCOLS] = natural[c] * factor_out

    f1.wait_send()
    for cp in f2 + ma + mb:
        cp.wait_send()

    @pl.loop(0, 4)
    def _(qq):
        m1_copy(qq).wait_send()

    for s in range(SLOTS):
        @pl.when(rest != s)
        def _():
            f3_copy(s, rest).wait_send()

    @pl.when(is_a)
    def _():
        @pl.loop(0, owners)
        def _(i):
            @pl.when(i != slot)
            def _():
                a_copy(i, 0).wait_send()

    @pl.when(is_g)
    def _():
        @pl.loop(0, 4 * rest_n)
        def _(i):
            @pl.when(not_me(i))
            def _():
                g_copy(i, 0).wait_send()

    @pl.loop(0, owners)
    def _(k):
        @pl.when(q * owners + k != me)
        def _():
            fin_copy(k, 0).wait_send()

    @pl.loop(0, devices)
    def _(d):
        @pl.when(d != me)
        def _():
            q_copy(d, 0).wait_send()


def per_device(acts, cotangents, groups, width):
    tokens = acts.shape[0]
    devices = groups * width
    rest_n = devices // 8
    owners = devices // 4
    rows = D // devices
    padded = (rows + 15) // 16 * 16
    blk = (BLK, BLK)
    sems = [1, 1, 3, 3, SLOTS, rest_n, 4, 4, 4, 4, 2, 2, max(owners, 4 * rest_n), QBLK + CBLK,
            owners, owners, devices, devices]
    vm = pltpu.VMEM
    return pl.pallas_call(
        functools.partial(kernel, groups, width, tokens * devices, rows),
        out_shape=jax.ShapeDtypeStruct((rows, R), F32),
        in_specs=[pl.BlockSpec(memory_space=pltpu.VMEM)] * 2,
        out_specs=pl.BlockSpec(memory_space=pltpu.VMEM),
        scratch_shapes=[
            vm((NA, BLK, tokens), BF16),
            vm((2, 4, SLOTS) + blk, BF16),
            vm((4, SLOTS) + blk, BF16),
            vm((3, SLOTS) + blk, BF16),
            vm((3, SLOTS) + blk, BF16),
            vm((SLOTS,) + blk, BF16),
            vm((rest_n,) + blk, BF16),
            vm((4, QROWS, CCOLS), BF16),
            vm((4, QROWS, CCOLS), BF16),
            vm((4, QROWS, CCOLS), BF16),
            vm((4, HALF, CCOLS), BF16),
            vm((4, HALF, CCOLS), BF16),
            vm((2, HALF, CCOLS), BF16),
            vm((QROWS, CCOLS), BF16),
            vm(blk, BF16),
            vm((QBLK,) + blk, BF16),
            vm((CBLK,) + blk, BF16),
            vm((QROWS, CCOLS), F32),
            vm((owners, padded, CCOLS), BF16),
            vm((owners, padded, CCOLS), BF16),
            vm((8, 128), F32),
            vm((devices, 8, 128), F32),
        ] + [pltpu.SemaphoreType.DMA((n,)) for n in sems],
        compiler_params=pltpu.CompilerParams(
            collective_id=0, has_side_effects=True, vmem_limit_bytes=48 * 1024 * 1024
        ),
    )(acts, cotangents)


def solution(mesh):
    groups, width = mesh.shape["grp"], mesh.shape["dp"]
    spec = P(("grp", "dp"), None)
    return jax.shard_map(
        functools.partial(per_device, groups=groups, width=width),
        mesh=mesh, in_specs=(spec, spec), out_specs=spec, check_vma=False,
    )
```

```python
import functools

import jax
import jax.numpy as jnp
from jax import lax
from jax.experimental import pallas as pl
from jax.experimental.pallas import tpu as pltpu
from jax.sharding import PartitionSpec as P

D = 2560
R = 768
BLK = 128
ITERS = 8
NA = D // BLK
NG = R // BLK
QROWS = D // 4
QBLK = QROWS // BLK
HALF = QROWS // 2
CCOLS = R // 2
CBLK = CCOLS // BLK
SLOTS = 4
MESH = pl.DeviceIdType.MESH
F32 = jnp.float32
BF16 = jnp.bfloat16


def dot(a, b):
    return jnp.dot(a, b, preferred_element_type=F32)


def dot_t(a, b):
    return lax.dot_general(a, b, (((0,), (0,)), ((), ())), preferred_element_type=F32)


def split(a):
    hi = a.astype(BF16)
    return hi, (a - hi.astype(F32)).astype(BF16)


def dot3(a, b):
    ah, al = split(a)
    bh, bl = split(b)
    return dot(jnp.concatenate([ah, ah, al], axis=1), jnp.concatenate([bh, bl, bh], axis=0))


def kernel(
    groups, width, total, rows,
    x_hbm, g_hbm, out_ref,
    x_ref, g_ref, xt, fpart, f1recv, f2send, f2recv, f3send, f3recv,
    m1send, m1recv, macc, m2a, m2s, m2b, mq,
    zsend, zrecv, inv_own, inv_a, inv_g, nat, fin_send, fin_recv, qsend, q1recv, q2recv,
    in_sem,
    f1_ss, f1_rs, f2_ss, f2_rs, f3_ss, f3_rs, m1_ss, m1_rs, ma_ss, ma_rs,
    mb_ss, mb_rs, z_ss, z_rs, inv_ss, inv_rs, fin_ss, fin_rs, q1_ss, q1_rs, q2_ss, q2_rs,
):
    devices = groups * width
    rest_n = devices // 8
    owners = devices // 4
    zslots = zsend.shape[1]
    pieces = fin_send.shape[0] // zslots
    dp_rest = width // 4
    gi = lax.axis_index("grp")
    di = lax.axis_index("dp")
    me = gi * width + di
    core = lax.rem(di, 2)
    x = lax.rem(lax.div(di, 2), 2)
    y = lax.rem(gi, 2)
    q = 2 * y + x
    rest = lax.div(gi, 2) * dp_rest + lax.div(di, 4)

    def at(yy, xx, zz, cc):
        return (
            lax.div(zz, dp_rest) * 2 + yy,
            lax.rem(zz, dp_rest) * 4 + xx * 2 + cc,
        )

    def linear(d):
        return (lax.div(d, width), lax.rem(d, width))

    def rcopy(src, dst, ss, rs, dev):
        return pltpu.make_async_remote_copy(
            src_ref=src, dst_ref=dst, send_sem=ss, recv_sem=rs,
            device_id=dev, device_id_type=MESH,
        )

    g_in = pltpu.make_async_copy(g_hbm, g_ref, in_sem.at[4])
    g_in.start()
    x_in = []
    for i in range(4):
        cols = pl.ds(i * QROWS, QROWS)
        x_in.append(pltpu.make_async_copy(x_hbm.at[:, cols], x_ref.at[:, cols], in_sem.at[i]))
        x_in[i].start()

    barrier = pltpu.get_barrier_semaphore()

    @pl.loop(0, devices)
    def _(d):
        @pl.when(d != me)
        def _():
            pl.semaphore_signal(barrier, inc=1, device_id=linear(d), device_id_type=MESH)

    zero = jnp.zeros((BLK, BLK), BF16)
    g_in.wait()
    for c in range(NG):
        gb = g_ref[:, c * BLK:(c + 1) * BLK]
        fg = dot_t(gb, gb).astype(BF16)
        if c < 4:
            fpart[1, c, 2] = fg
        else:
            fpart[0, c - 4, 3] = fg
    for c in range(4):
        fpart[1, c, 3] = zero
        if c >= NG - 4:
            fpart[0, c, 3] = zero

    for qq in range(4):
        x_in[qq].wait()
        for t in range(QBLK):
            b = qq * QBLK + t
            xb = x_ref[:, b * BLK:(b + 1) * BLK]
            xbt = xb.T
            xt[b] = xbt
            fpart[t % 2, qq, t // 2] = dot(xbt, xb).astype(BF16)

    pl.semaphore_wait(barrier, devices - 1)
    other = at(y, x, rest, 1 - core)
    f1 = rcopy(fpart.at[1 - core], f1recv, f1_ss.at[0], f1_rs.at[0], other)
    f1.start()

    g_other = g_ref[:, pl.ds(pl.multiple_of((1 - core) * CCOLS, BLK), CCOLS)]

    def m1_copy(qq):
        return rcopy(m1send.at[qq], m1recv.at[qq], m1_ss.at[qq], m1_rs.at[qq], other)

    @pl.loop(0, 4)
    def _(qq):
        for t in range(QBLK):
            m1send[qq, t * BLK:(t + 1) * BLK, :] = dot(xt[qq * QBLK + t], g_other).astype(BF16)
        m1_copy(qq).start()

    f1.wait_recv()

    def f1_sum(qq, s):
        return fpart[core, qq, s].astype(F32) + f1recv[qq, s].astype(F32)

    chips = [(y, 1 - x), (1 - y, x), (1 - y, 1 - x)]
    f2 = []
    for k, (yy, xx) in enumerate(chips):
        qq = 2 * yy + xx
        for s in range(SLOTS):
            f2send[k, s] = f1_sum(qq, s).astype(BF16)
        c2 = rcopy(f2send.at[k], f2recv.at[k], f2_ss.at[k], f2_rs.at[k], at(yy, xx, rest, core))
        c2.start()
        f2.append(c2)

    g_mine = g_ref[:, pl.ds(pl.multiple_of(core * CCOLS, BLK), CCOLS)]

    @pl.loop(0, 4)
    def _(qq):
        m1_copy(qq).wait_recv()
        for t in range(QBLK):
            part = dot(xt[qq * QBLK + t], g_mine)
            sl = slice(t * BLK, (t + 1) * BLK)
            macc[qq, sl, :] = (part + m1recv[qq, sl, :].astype(F32)).astype(BF16)

    at_x = at(y, 1 - x, rest, core)
    at_y = at(1 - y, x, rest, core)
    ma = []
    for i in range(2):
        for h in range(2):
            k = 2 * h + i
            quarter = 2 * i + (1 - x) if h == 0 else 2 * (1 - y) + i
            ca = rcopy(
                macc.at[quarter, pl.ds(h * HALF, HALF)], m2a.at[k],
                ma_ss.at[k], ma_rs.at[k], at_x if h == 0 else at_y,
            )
            ca.start()
            ma.append(ca)

    for c2 in f2:
        c2.wait_recv()
    for s in range(SLOTS):
        f = f1_sum(q, s)
        for k in range(3):
            f = f + f2recv[k, s].astype(F32)
        f3send[s] = f.astype(BF16)

    def f3_copy(s, src):
        return rcopy(f3send.at[s], f3recv.at[src], f3_ss.at[s], f3_rs.at[src], at(y, x, s, core))

    for s in range(SLOTS):
        @pl.when(rest != s)
        def _():
            f3_copy(s, rest).start()

    f3recv[rest] = f3send[lax.rem(rest, SLOTS)]

    @pl.when(rest < SLOTS)
    def _():
        @pl.loop(0, rest_n)
        def _(z):
            @pl.when(z != rest)
            def _():
                f3_copy(0, z).wait_recv()

    if rest_n > SLOTS:
        @pl.when(rest >= SLOTS)
        def _():
            @pl.loop(0, rest_n)
            def _(z):
                f3recv[z] = zero

    factor = f3recv[0].astype(F32)
    for z in range(1, rest_n):
        factor = factor + f3recv[z].astype(F32)
    factor = factor * (1.0 / total)

    eye = (
        lax.broadcasted_iota(jnp.int32, (BLK, BLK), 0)
        == lax.broadcasted_iota(jnp.int32, (BLK, BLK), 1)
    ).astype(F32)
    trace = jnp.sum(jnp.sum(factor * eye, axis=1, keepdims=True), axis=0, keepdims=True)
    damped = factor + (0.1 * (trace / BLK + 1e-06)) * eye
    peak = jnp.max(jnp.sum(jnp.abs(damped), axis=1, keepdims=True), axis=0, keepdims=True)
    scale = 1.0 / peak
    approx = scale * (2.0 * eye - scale * damped)
    for _ in range(ITERS - 5):
        approx = dot3(approx, 2.0 * eye - dot3(damped, approx))

    for ca in ma:
        ca.wait_recv()
    for i in range(2):
        for h in range(2):
            k = 2 * h + i
            quarter = 2 * i + x if h == 0 else 2 * y + i
            m2s[k] = (
                macc[quarter, h * HALF:(h + 1) * HALF, :].astype(F32) + m2a[k].astype(F32)
            ).astype(BF16)
    mb = [
        rcopy(m2s.at[1 - y], m2b.at[0], mb_ss.at[0], mb_rs.at[0], at_y),
        rcopy(m2s.at[2 + 1 - x], m2b.at[1], mb_ss.at[1], mb_rs.at[1], at_x),
    ]
    for cb in mb:
        cb.start()

    for _ in range(4):
        approx = dot3(approx, 2.0 * eye - dot3(damped, approx))
    inv_own[...] = approx.astype(BF16)

    slot = 2 * rest + core
    is_a = slot < QBLK
    is_g = jnp.logical_or(slot == QBLK, jnp.logical_and(slot == QBLK + 1, q < NG - 4))
    gidx = (slot - QBLK) * 4 + q
    ghalf = lax.div(gidx, CBLK)

    def a_copy(i, t):
        return rcopy(
            inv_own, inv_a.at[t], inv_ss.at[i], inv_rs.at[t],
            at(y, x, lax.div(i, 2), lax.rem(i, 2)),
        )

    def g_dev(i):
        chip = lax.div(i, rest_n)
        return at(lax.div(chip, 2), lax.rem(chip, 2), lax.rem(i, rest_n), ghalf)

    def g_copy(i, c):
        return rcopy(inv_own, inv_g.at[c], inv_ss.at[i], inv_rs.at[QBLK + c], g_dev(i))

    def not_me(i):
        gg, dd = g_dev(i)
        return gg * width + dd != me

    @pl.when(is_a)
    def _():
        @pl.loop(0, owners)
        def _(i):
            @pl.when(i != slot)
            def _():
                a_copy(i, slot).start()
        inv_a[slot] = inv_own[...]

    @pl.when(is_g)
    def _():
        @pl.loop(0, 4 * rest_n)
        def _(i):
            @pl.when(not_me(i))
            def _():
                g_copy(i, lax.rem(gidx, CBLK)).start()

        @pl.when(ghalf == core)
        def _():
            inv_g[lax.rem(gidx, CBLK)] = inv_own[...]

    for cb in mb:
        cb.wait_recv()
    for h in range(2):
        kept = m2s[y] if h == 0 else m2s[2 + x]
        mq[h * HALF:(h + 1) * HALF, :] = (
            (kept.astype(F32) + m2b[h].astype(F32)) * (1.0 / total)
        ).astype(BF16)

    for i in range(zslots * rest_n):
        t, c = divmod(i, CBLK)
        tile = zero if t >= QBLK else mq[t * BLK:(t + 1) * BLK, c * BLK:(c + 1) * BLK]
        zsend[i % rest_n, i // rest_n] = tile

    def z_copy(dst, src):
        return rcopy(zsend.at[dst], zrecv.at[src], z_ss.at[dst], z_rs.at[src], at(y, x, dst, core))

    @pl.loop(0, rest_n)
    def _(z):
        @pl.when(z != rest)
        def _():
            z_copy(z, rest).start()

    zrecv[rest] = zsend[rest]

    for c in range(CBLK):
        @pl.when(jnp.logical_not(jnp.logical_and(is_g, gidx == core * CBLK + c)))
        def _():
            g_copy(0, c).wait_recv()
    for t in range(QBLK):
        @pl.when(slot != t)
        def _():
            a_copy(0, t).wait_recv()

    @pl.loop(0, rest_n)
    def _(z):
        @pl.when(z != rest)
        def _():
            z_copy(0, z).wait_recv()

    square = jnp.zeros((1, 1), F32)
    for k in range(zslots):
        tile = k * rest_n + rest
        m = zrecv[0, k].astype(F32)
        for z in range(1, rest_n):
            m = m + zrecv[z, k].astype(F32)
        left = dot_t(inv_a[jnp.minimum(lax.div(tile, CBLK), QBLK - 1)], m.astype(BF16))
        hi, lo = split(left)
        ginv = inv_g[lax.rem(tile, CBLK)]
        part = dot(hi, ginv) + dot(lo, ginv)
        nat[k] = part
        square = square + jnp.sum(
            jnp.sum(part * part, axis=0, keepdims=True), axis=1, keepdims=True
        )
    qsend[0] = jnp.broadcast_to(square, (8, 128))

    def q1_copy(p, src):
        return rcopy(
            qsend.at[0], q1recv.at[src], q1_ss.at[p], q1_rs.at[src],
            at(lax.div(p, 4), lax.rem(lax.div(p, 2), 2), rest, lax.rem(p, 2)),
        )

    def q2_copy(z, src):
        return rcopy(qsend.at[1], q2recv.at[src], q2_ss.at[z], q2_rs.at[src], at(y, x, z, core))

    plane = 2 * q + core

    def others(n, mine, body):
        @pl.loop(0, n)
        def _(p):
            @pl.when(p != mine)
            def _():
                body(p)

    others(8, plane, lambda p: q1_copy(p, plane).start())
    q1recv[plane] = qsend[0]

    def each_piece(body):
        for i in range(QBLK * CBLK):
            t, c = divmod(i, CBLK)

            @pl.when(rest == i % rest_n)
            def _():
                first = t * BLK // rows
                for k in range(first, min(owners, ((t + 1) * BLK + rows - 1) // rows)):
                    lo, hi = max(t * BLK, k * rows), min((t + 1) * BLK, (k + 1) * rows)
                    late = 0 if lo == k * rows else 1
                    body(i, t, c, k, lo, hi, late, i // rest_n * pieces + k - first)

    def fin_copy(j, c, late, k):
        return rcopy(
            fin_send.at[j], fin_recv.at[core * CBLK + c, late], fin_ss.at[j],
            fin_rs.at[2 * (core * CBLK + c) + late], linear(q * owners + k),
        )

    def send_piece(i, t, c, k, lo, hi, late, j):
        parts = [nat[i // rest_n, lo - t * BLK:hi - t * BLK, :]]
        if lo > k * rows:
            parts.insert(0, jnp.zeros((lo - k * rows, BLK), F32))
        tail = fin_send.shape[1] - (hi - k * rows)
        if tail:
            parts.append(jnp.zeros((tail, BLK), F32))
        fin_send[j] = (jnp.concatenate(parts, axis=0) if len(parts) > 1 else parts[0]).astype(BF16)

        @pl.when(q * owners + k != me)
        def _():
            fin_copy(j, c, late, k).start()

        @pl.when(q * owners + k == me)
        def _():
            fin_recv[core * CBLK + c, late] = fin_send[j]

    each_piece(send_piece)

    others(8, plane, lambda p: q1_copy(0, p).wait_recv())
    qsend[1] = jnp.sum(q1recv[...], axis=0)
    others(rest_n, rest, lambda z: q2_copy(z, rest).start())
    q2recv[rest] = qsend[1]

    k_me = lax.rem(me, owners)
    t_me = lax.div(k_me * rows, BLK)
    straddles = lax.div(k_me * rows + rows - 1, BLK) > t_me
    mine_here = lax.div(me, owners) == q
    for late in range(2):
        for c in range(NG):
            from_me = jnp.logical_and(
                jnp.logical_and(mine_here, core == c // CBLK),
                lax.rem(CBLK * (t_me + late) + c % CBLK, rest_n) == rest,
            )
            incoming = jnp.logical_not(from_me)
            if late:
                incoming = jnp.logical_and(straddles, incoming)

                @pl.when(jnp.logical_not(straddles))
                def _():
                    fin_recv[c, 1] = jnp.zeros(fin_recv.shape[2:], BF16)

            @pl.when(incoming)
            def _():
                pltpu.make_async_remote_copy(
                    src_ref=fin_send.at[0], dst_ref=fin_recv.at[c, late], send_sem=fin_ss.at[0],
                    recv_sem=fin_rs.at[2 * c + late], device_id=other, device_id_type=MESH,
                ).wait_recv()

    others(rest_n, rest, lambda z: q2_copy(0, z).wait_recv())
    quad = jnp.sum(q2recv[...], axis=0)[:1, :1] / (D * R)
    factor_out = lax.rsqrt(quad + 1e-06)
    for c in range(NG):
        natural = fin_recv[c, 0].astype(F32) + fin_recv[c, 1].astype(F32)
        out_ref[:, c * BLK:(c + 1) * BLK] = natural[:rows, :] * factor_out

    f1.wait_send()
    for cp in f2 + ma + mb:
        cp.wait_send()

    @pl.loop(0, 4)
    def _(qq):
        m1_copy(qq).wait_send()

    for s in range(SLOTS):
        @pl.when(rest != s)
        def _():
            f3_copy(s, rest).wait_send()

    @pl.when(is_a)
    def _():
        @pl.loop(0, owners)
        def _(i):
            @pl.when(i != slot)
            def _():
                a_copy(i, 0).wait_send()

    @pl.when(is_g)
    def _():
        @pl.loop(0, 4 * rest_n)
        def _(i):
            @pl.when(not_me(i))
            def _():
                g_copy(i, 0).wait_send()

    others(rest_n, rest, lambda z: z_copy(z, 0).wait_send())
    others(8, plane, lambda p: q1_copy(p, 0).wait_send())
    others(rest_n, rest, lambda z: q2_copy(z, 0).wait_send())

    def wait_piece(i, t, c, k, lo, hi, late, j):
        @pl.when(q * owners + k != me)
        def _():
            fin_copy(j, c, late, k).wait_send()

    each_piece(wait_piece)


def per_device(acts, cotangents, groups, width):
    tokens = acts.shape[0]
    devices = groups * width
    rest_n = devices // 8
    owners = devices // 4
    rows = D // devices
    padded = (rows + 15) // 16 * 16
    blk = (BLK, BLK)
    zslots = (QBLK * CBLK + rest_n - 1) // rest_n
    pieces = max(
        ((t + 1) * BLK + rows - 1) // rows - t * BLK // rows for t in range(QBLK)
    )
    sems = [5, 1, 1, 3, 3, SLOTS, rest_n, 4, 4, 4, 4, 2, 2, rest_n, rest_n, max(owners, 4 * rest_n),
            QBLK + CBLK, zslots * pieces, 2 * NG, 8, 8, rest_n, rest_n]
    vm = pltpu.VMEM
    return pl.pallas_call(
        functools.partial(kernel, groups, width, tokens * devices, rows),
        out_shape=jax.ShapeDtypeStruct((rows, R), F32),
        in_specs=[pl.BlockSpec(memory_space=pl.ANY)] * 2,
        out_specs=pl.BlockSpec(memory_space=pltpu.VMEM),
        scratch_shapes=[
            vm((tokens, D), BF16),
            vm((tokens, R), BF16),
            vm((NA, BLK, tokens), BF16),
            vm((2, 4, SLOTS) + blk, BF16),
            vm((4, SLOTS) + blk, BF16),
            vm((3, SLOTS) + blk, BF16),
            vm((3, SLOTS) + blk, BF16),
            vm((SLOTS,) + blk, BF16),
            vm((rest_n,) + blk, BF16),
            vm((4, QROWS, CCOLS), BF16),
            vm((4, QROWS, CCOLS), BF16),
            vm((4, QROWS, CCOLS), BF16),
            vm((4, HALF, CCOLS), BF16),
            vm((4, HALF, CCOLS), BF16),
            vm((2, HALF, CCOLS), BF16),
            vm((QROWS, CCOLS), BF16),
            vm((rest_n, zslots) + blk, BF16),
            vm((rest_n, zslots) + blk, BF16),
            vm(blk, BF16),
            vm((QBLK,) + blk, BF16),
            vm((CBLK,) + blk, BF16),
            vm((zslots,) + blk, F32),
            vm((zslots * pieces, padded, BLK), BF16),
            vm((NG, 2, padded, BLK), BF16),
            vm((2, 8, 128), F32),
            vm((8, 8, 128), F32),
            vm((rest_n, 8, 128), F32),
        ] + [pltpu.SemaphoreType.DMA((n,)) for n in sems],
        compiler_params=pltpu.CompilerParams(
            collective_id=0, has_side_effects=True, vmem_limit_bytes=48 * 1024 * 1024
        ),
    )(acts, cotangents)


def solution(mesh):
    groups, width = mesh.shape["grp"], mesh.shape["dp"]
    spec = P(("grp", "dp"), None)
    return jax.shard_map(
        functools.partial(per_device, groups=groups, width=width),
        mesh=mesh, in_specs=(spec, spec), out_specs=spec, check_vma=False,
    )
```

```python
import functools

import jax
import jax.numpy as jnp
from jax import lax
from jax.experimental import pallas as pl
from jax.experimental.pallas import tpu as pltpu
from jax.sharding import PartitionSpec as P

D = 2560
R = 768
BLK = 128
ITERS = 8
NA = D // BLK
NG = R // BLK
QROWS = D // 4
QBLK = QROWS // BLK
HALF = QROWS // 2
CCOLS = R // 2
CBLK = CCOLS // BLK
SLOTS = 4
MESH = pl.DeviceIdType.MESH
F32 = jnp.float32
BF16 = jnp.bfloat16


def dot(a, b):
    return jnp.dot(a, b, preferred_element_type=F32)


def dot_t(a, b):
    return lax.dot_general(a, b, (((0,), (0,)), ((), ())), preferred_element_type=F32)


def split(a):
    hi = a.astype(BF16)
    return hi, (a - hi.astype(F32)).astype(BF16)


def dot3(a, b):
    ah, al = split(a)
    bh, bl = split(b)
    return dot(jnp.concatenate([ah, ah, al], axis=1), jnp.concatenate([bh, bl, bh], axis=0))


def kernel(
    groups, width, total, rows,
    x_hbm, g_hbm, out_ref,
    x_ref, g_ref, xt, fpart, f1recv, f2send, f2recv, f3send, f3recv,
    m1send, m1recv, macc, m2a, m2s, m2b, mq,
    zsend, zrecv, inv_own, inv_a, inv_g, nat, fin_send, fin_recv, qsend, q1recv, q2recv,
    in_sem,
    f1_ss, f1_rs, f2_ss, f2_rs, f3_ss, f3_rs, m1_ss, m1_rs, ma_ss, ma_rs,
    mb_ss, mb_rs, z_ss, z_rs, inv_ss, inv_rs, fin_ss, fin_rs, q1_ss, q1_rs, q2_ss, q2_rs,
):
    devices = groups * width
    rest_n = devices // 8
    owners = devices // 4
    half_n = devices // 2
    zslots = zsend.shape[1]
    pieces = fin_send.shape[0] // zslots
    dp_rest = width // 4
    gi = lax.axis_index("grp")
    di = lax.axis_index("dp")
    me = gi * width + di
    core = lax.rem(di, 2)
    x = lax.rem(lax.div(di, 2), 2)
    y = lax.rem(gi, 2)
    q = 2 * y + x
    rest = lax.div(gi, 2) * dp_rest + lax.div(di, 4)

    def at(yy, xx, zz, cc):
        return (
            lax.div(zz, dp_rest) * 2 + yy,
            lax.rem(zz, dp_rest) * 4 + xx * 2 + cc,
        )

    def linear(d):
        return (lax.div(d, width), lax.rem(d, width))

    def rcopy(src, dst, ss, rs, dev):
        return pltpu.make_async_remote_copy(
            src_ref=src, dst_ref=dst, send_sem=ss, recv_sem=rs,
            device_id=dev, device_id_type=MESH,
        )

    g_in = pltpu.make_async_copy(g_hbm, g_ref, in_sem.at[4])
    g_in.start()
    x_in = []
    for i in range(4):
        cols = pl.ds(i * QROWS, QROWS)
        x_in.append(pltpu.make_async_copy(x_hbm.at[:, cols], x_ref.at[:, cols], in_sem.at[i]))
        x_in[i].start()

    barrier = pltpu.get_barrier_semaphore()

    def greet(dev):
        pl.semaphore_signal(barrier, inc=1, device_id=dev, device_id_type=MESH)

    greet(at(y, x, rest, 1 - core))
    for yy, xx in ((y, 1 - x), (1 - y, x), (1 - y, 1 - x)):
        greet(at(yy, xx, rest, core))

    @pl.loop(0, rest_n)
    def _(z):
        @pl.when(z != rest)
        def _():
            greet(at(y, x, z, core))

    zero = jnp.zeros((BLK, BLK), BF16)
    g_in.wait()
    for c in range(NG):
        gb = g_ref[:, c * BLK:(c + 1) * BLK]
        fg = dot_t(gb, gb).astype(BF16)
        if c < 4:
            fpart[1, c, 2] = fg
        else:
            fpart[0, c - 4, 3] = fg
    for c in range(4):
        fpart[1, c, 3] = zero
        if c >= NG - 4:
            fpart[0, c, 3] = zero

    for part in range(4):
        x_in[part].wait()
        for b in range(part * QBLK, (part + 1) * QBLK):
            qq, t = b // (2 * QBLK) * 2 + b % 2, b % (2 * QBLK) // 2
            xb = x_ref[:, b * BLK:(b + 1) * BLK]
            xbt = xb.T
            xt[qq * QBLK + t] = xbt
            fpart[t % 2, qq, t // 2] = dot(xbt, xb).astype(BF16)

    pl.semaphore_wait(barrier, rest_n + 3)
    other = at(y, x, rest, 1 - core)
    f1 = rcopy(fpart.at[1 - core], f1recv, f1_ss.at[0], f1_rs.at[0], other)
    f1.start()

    g_other = g_ref[:, pl.ds(pl.multiple_of((1 - core) * CCOLS, BLK), CCOLS)]

    def m1_copy(qq):
        return rcopy(m1send.at[qq], m1recv.at[qq], m1_ss.at[qq], m1_rs.at[qq], other)

    @pl.loop(0, 4)
    def _(qq):
        for t in range(QBLK):
            m1send[qq, t * BLK:(t + 1) * BLK, :] = dot(xt[qq * QBLK + t], g_other).astype(BF16)
        m1_copy(qq).start()

    f1.wait_recv()

    def f1_sum(qq, s):
        return fpart[core, qq, s].astype(F32) + f1recv[qq, s].astype(F32)

    chips = [(y, 1 - x), (1 - y, x), (1 - y, 1 - x)]
    f2 = []
    for k, (yy, xx) in enumerate(chips):
        qq = 2 * yy + xx
        for s in range(SLOTS):
            f2send[k, s] = f1_sum(qq, s).astype(BF16)
        c2 = rcopy(f2send.at[k], f2recv.at[k], f2_ss.at[k], f2_rs.at[k], at(yy, xx, rest, core))
        c2.start()
        f2.append(c2)

    g_mine = g_ref[:, pl.ds(pl.multiple_of(core * CCOLS, BLK), CCOLS)]

    @pl.loop(0, 4)
    def _(qq):
        m1_copy(qq).wait_recv()
        for t in range(QBLK):
            part = dot(xt[qq * QBLK + t], g_mine)
            sl = slice(t * BLK, (t + 1) * BLK)
            macc[qq, sl, :] = (part + m1recv[qq, sl, :].astype(F32)).astype(BF16)

    at_x = at(y, 1 - x, rest, core)
    at_y = at(1 - y, x, rest, core)
    ma = []
    for i in range(2):
        for h in range(2):
            k = 2 * h + i
            quarter = 2 * i + (1 - x) if h == 0 else 2 * (1 - y) + i
            ca = rcopy(
                macc.at[quarter, pl.ds(h * HALF, HALF)], m2a.at[k],
                ma_ss.at[k], ma_rs.at[k], at_x if h == 0 else at_y,
            )
            ca.start()
            ma.append(ca)

    for c2 in f2:
        c2.wait_recv()
    for s in range(SLOTS):
        f = f1_sum(q, s)
        for k in range(3):
            f = f + f2recv[k, s].astype(F32)
        f3send[s] = f.astype(BF16)

    def f3_copy(s, src):
        return rcopy(f3send.at[s], f3recv.at[src], f3_ss.at[s], f3_rs.at[src], at(y, x, s, core))

    for s in range(SLOTS):
        @pl.when(rest != s)
        def _():
            f3_copy(s, rest).start()

    f3recv[rest] = f3send[lax.rem(rest, SLOTS)]

    @pl.when(rest < SLOTS)
    def _():
        @pl.loop(0, rest_n)
        def _(z):
            @pl.when(z != rest)
            def _():
                f3_copy(0, z).wait_recv()

    if rest_n > SLOTS:
        @pl.when(rest >= SLOTS)
        def _():
            @pl.loop(0, rest_n)
            def _(z):
                f3recv[z] = zero

    factor = f3recv[0].astype(F32)
    for z in range(1, rest_n):
        factor = factor + f3recv[z].astype(F32)
    factor = factor * (1.0 / total)

    eye = (
        lax.broadcasted_iota(jnp.int32, (BLK, BLK), 0)
        == lax.broadcasted_iota(jnp.int32, (BLK, BLK), 1)
    ).astype(F32)
    trace = jnp.sum(jnp.sum(factor * eye, axis=1, keepdims=True), axis=0, keepdims=True)
    damped = factor + (0.1 * (trace / BLK + 1e-06)) * eye
    peak = jnp.max(jnp.sum(jnp.abs(damped), axis=1, keepdims=True), axis=0, keepdims=True)
    scale = 1.0 / peak
    approx = scale * (2.0 * eye - scale * damped)
    for _ in range(ITERS - 5):
        approx = dot3(approx, 2.0 * eye - dot3(damped, approx))

    for ca in ma:
        ca.wait_recv()
    for i in range(2):
        for h in range(2):
            k = 2 * h + i
            quarter = 2 * i + x if h == 0 else 2 * y + i
            m2s[k] = (
                macc[quarter, h * HALF:(h + 1) * HALF, :].astype(F32) + m2a[k].astype(F32)
            ).astype(BF16)
    mb = [
        rcopy(m2s.at[1 - y], m2b.at[0], mb_ss.at[0], mb_rs.at[0], at_y),
        rcopy(m2s.at[2 + 1 - x], m2b.at[1], mb_ss.at[1], mb_rs.at[1], at_x),
    ]
    for cb in mb:
        cb.start()

    for _ in range(4):
        approx = dot3(approx, 2.0 * eye - dot3(damped, approx))
    inv_own[...] = approx.astype(BF16)

    slot = 2 * rest + core
    is_a = slot < QBLK
    is_g = jnp.logical_or(slot == QBLK, jnp.logical_and(slot == QBLK + 1, q < NG - 4))
    gidx = (slot - QBLK) * 4 + q
    ghalf = lax.div(gidx, CBLK)

    def a_copy(i, t):
        return rcopy(
            inv_own, inv_a.at[t], inv_ss.at[i], inv_rs.at[t],
            at(y, x, lax.div(i, 2), lax.rem(i, 2)),
        )

    def g_dev(i):
        chip = lax.div(i, rest_n)
        return at(lax.div(chip, 2), lax.rem(chip, 2), lax.rem(i, rest_n), ghalf)

    def g_copy(i, c):
        return rcopy(inv_own, inv_g.at[c], inv_ss.at[i], inv_rs.at[QBLK + c], g_dev(i))

    def not_me(i):
        gg, dd = g_dev(i)
        return gg * width + dd != me

    @pl.when(is_a)
    def _():
        @pl.loop(0, owners)
        def _(i):
            @pl.when(i != slot)
            def _():
                a_copy(i, slot).start()
        inv_a[slot] = inv_own[...]

    @pl.when(is_g)
    def _():
        @pl.loop(0, 4 * rest_n)
        def _(i):
            @pl.when(not_me(i))
            def _():
                g_copy(i, lax.rem(gidx, CBLK)).start()

        @pl.when(ghalf == core)
        def _():
            inv_g[lax.rem(gidx, CBLK)] = inv_own[...]

    for cb in mb:
        cb.wait_recv()
    for h in range(2):
        kept = m2s[y] if h == 0 else m2s[2 + x]
        mq[h * HALF:(h + 1) * HALF, :] = (
            (kept.astype(F32) + m2b[h].astype(F32)) * (1.0 / total)
        ).astype(BF16)

    for i in range(zslots * rest_n):
        t, c = divmod(i, CBLK)
        tile = zero if t >= QBLK else mq[t * BLK:(t + 1) * BLK, c * BLK:(c + 1) * BLK]
        zsend[i // zslots, i % zslots] = tile

    def z_copy(dst, src):
        return rcopy(zsend.at[dst], zrecv.at[src], z_ss.at[dst], z_rs.at[src], at(y, x, dst, core))

    @pl.loop(0, rest_n)
    def _(z):
        @pl.when(z != rest)
        def _():
            z_copy(z, rest).start()

    zrecv[rest] = zsend[rest]

    for c in range(CBLK):
        @pl.when(jnp.logical_not(jnp.logical_and(is_g, gidx == core * CBLK + c)))
        def _():
            g_copy(0, c).wait_recv()
    for t in range(QBLK):
        @pl.when(slot != t)
        def _():
            a_copy(0, t).wait_recv()

    @pl.loop(0, rest_n)
    def _(z):
        @pl.when(z != rest)
        def _():
            z_copy(0, z).wait_recv()

    square = jnp.zeros((1, 1), F32)
    for k in range(zslots):
        tile = rest * zslots + k
        m = zrecv[0, k].astype(F32)
        for z in range(1, rest_n):
            m = m + zrecv[z, k].astype(F32)
        left = dot_t(inv_a[jnp.minimum(lax.div(tile, CBLK), QBLK - 1)], m.astype(BF16))
        hi, lo = split(left)
        ginv = inv_g[lax.rem(tile, CBLK)]
        part = dot(hi, ginv) + dot(lo, ginv)
        nat[k] = part
        square = square + jnp.sum(
            jnp.sum(part * part, axis=0, keepdims=True), axis=1, keepdims=True
        )
    qsend[0] = jnp.broadcast_to(square, (8, 128))

    def q1_copy(p, src):
        return rcopy(
            qsend.at[0], q1recv.at[src], q1_ss.at[p], q1_rs.at[src],
            at(lax.div(p, 4), lax.rem(lax.div(p, 2), 2), rest, lax.rem(p, 2)),
        )

    def q2_copy(z, src):
        return rcopy(qsend.at[1], q2recv.at[src], q2_ss.at[z], q2_rs.at[src], at(y, x, z, core))

    plane = 2 * q + core

    def others(n, mine, body):
        @pl.loop(0, n)
        def _(p):
            @pl.when(p != mine)
            def _():
                body(p)

    others(8, plane, lambda p: q1_copy(p, plane).start())
    q1recv[plane] = qsend[0]

    def each_piece(body):
        for xx in range(2):
            for i in range(QBLK * CBLK):
                t, c = divmod(i, CBLK)
                top = (2 * t + xx) * BLK

                @pl.when(jnp.logical_and(x == xx, rest == i // zslots))
                def _():
                    first = top // rows
                    for k in range(first, (top + BLK + rows - 1) // rows):
                        lo, hi = max(top, k * rows), min(top + BLK, (k + 1) * rows)
                        late = 0 if lo == k * rows else 1
                        body(i % zslots, c, k, lo - k * rows, lo - top, hi - lo, late,
                             i % zslots * pieces + k - first)

    def fin_copy(j, c, late, k):
        return rcopy(
            fin_send.at[j], fin_recv.at[core * CBLK + c, late], fin_ss.at[j],
            fin_rs.at[2 * (core * CBLK + c) + late], linear(y * half_n + k),
        )

    def send_piece(slot_k, c, k, above, start, count, late, j):
        parts = [nat[slot_k, start:start + count, :]]
        if above:
            parts.insert(0, jnp.zeros((above, BLK), F32))
        tail = fin_send.shape[1] - above - count
        if tail:
            parts.append(jnp.zeros((tail, BLK), F32))
        fin_send[j] = (jnp.concatenate(parts, axis=0) if len(parts) > 1 else parts[0]).astype(BF16)

        @pl.when(y * half_n + k != me)
        def _():
            fin_copy(j, c, late, k).start()

        @pl.when(y * half_n + k == me)
        def _():
            fin_recv[core * CBLK + c, late] = fin_send[j]

    each_piece(send_piece)

    others(8, plane, lambda p: q1_copy(0, p).wait_recv())
    qsend[1] = jnp.sum(q1recv[...], axis=0)
    others(rest_n, rest, lambda z: q2_copy(z, rest).start())
    q2recv[rest] = qsend[1]

    k_me = lax.rem(me, half_n)
    t_me = lax.div(k_me * rows, BLK)
    straddles = lax.div(k_me * rows + rows - 1, BLK) > t_me
    mine_here = lax.div(me, half_n) == y
    for late in range(2):
        for c in range(NG):
            from_me = jnp.logical_and(
                jnp.logical_and(mine_here, core == c // CBLK),
                jnp.logical_and(
                    lax.rem(t_me + late, 2) == x,
                    lax.div(CBLK * lax.div(t_me + late, 2) + c % CBLK, zslots) == rest,
                ),
            )
            incoming = jnp.logical_not(from_me)
            if late:
                incoming = jnp.logical_and(straddles, incoming)

                @pl.when(jnp.logical_not(straddles))
                def _():
                    fin_recv[c, 1] = jnp.zeros(fin_recv.shape[2:], BF16)

            @pl.when(incoming)
            def _():
                pltpu.make_async_remote_copy(
                    src_ref=fin_send.at[0], dst_ref=fin_recv.at[c, late], send_sem=fin_ss.at[0],
                    recv_sem=fin_rs.at[2 * c + late], device_id=other, device_id_type=MESH,
                ).wait_recv()

    others(rest_n, rest, lambda z: q2_copy(0, z).wait_recv())
    quad = jnp.sum(q2recv[...], axis=0)[:1, :1] / (D * R)
    factor_out = lax.rsqrt(quad + 1e-06)
    for c in range(NG):
        natural = fin_recv[c, 0].astype(F32) + fin_recv[c, 1].astype(F32)
        out_ref[:, c * BLK:(c + 1) * BLK] = natural[:rows, :] * factor_out

    f1.wait_send()
    for cp in f2 + ma + mb:
        cp.wait_send()

    @pl.loop(0, 4)
    def _(qq):
        m1_copy(qq).wait_send()

    for s in range(SLOTS):
        @pl.when(rest != s)
        def _():
            f3_copy(s, rest).wait_send()

    @pl.when(is_a)
    def _():
        @pl.loop(0, owners)
        def _(i):
            @pl.when(i != slot)
            def _():
                a_copy(i, 0).wait_send()

    @pl.when(is_g)
    def _():
        @pl.loop(0, 4 * rest_n)
        def _(i):
            @pl.when(not_me(i))
            def _():
                g_copy(i, 0).wait_send()

    others(rest_n, rest, lambda z: z_copy(z, 0).wait_send())
    others(8, plane, lambda p: q1_copy(p, 0).wait_send())
    others(rest_n, rest, lambda z: q2_copy(z, 0).wait_send())

    def wait_piece(slot_k, c, k, above, start, count, late, j):
        @pl.when(y * half_n + k != me)
        def _():
            fin_copy(j, c, late, k).wait_send()

    each_piece(wait_piece)


def per_device(acts, cotangents, groups, width):
    tokens = acts.shape[0]
    devices = groups * width
    rest_n = devices // 8
    owners = devices // 4
    rows = D // devices
    padded = (rows + 15) // 16 * 16
    blk = (BLK, BLK)
    zslots = (QBLK * CBLK + rest_n - 1) // rest_n
    pieces = max(
        ((t + 1) * BLK + rows - 1) // rows - t * BLK // rows for t in range(2 * QBLK)
    )
    sems = [5, 1, 1, 3, 3, SLOTS, rest_n, 4, 4, 4, 4, 2, 2, rest_n, rest_n, max(owners, 4 * rest_n),
            QBLK + CBLK, zslots * pieces, 2 * NG, 8, 8, rest_n, rest_n]
    vm = pltpu.VMEM
    return pl.pallas_call(
        functools.partial(kernel, groups, width, tokens * devices, rows),
        out_shape=jax.ShapeDtypeStruct((rows, R), F32),
        in_specs=[pl.BlockSpec(memory_space=pl.ANY)] * 2,
        out_specs=pl.BlockSpec(memory_space=pltpu.VMEM),
        scratch_shapes=[
            vm((tokens, D), BF16),
            vm((tokens, R), BF16),
            vm((NA, BLK, tokens), BF16),
            vm((2, 4, SLOTS) + blk, BF16),
            vm((4, SLOTS) + blk, BF16),
            vm((3, SLOTS) + blk, BF16),
            vm((3, SLOTS) + blk, BF16),
            vm((SLOTS,) + blk, BF16),
            vm((rest_n,) + blk, BF16),
            vm((4, QROWS, CCOLS), BF16),
            vm((4, QROWS, CCOLS), BF16),
            vm((4, QROWS, CCOLS), BF16),
            vm((4, HALF, CCOLS), BF16),
            vm((4, HALF, CCOLS), BF16),
            vm((2, HALF, CCOLS), BF16),
            vm((QROWS, CCOLS), BF16),
            vm((rest_n, zslots) + blk, BF16),
            vm((rest_n, zslots) + blk, BF16),
            vm(blk, BF16),
            vm((QBLK,) + blk, BF16),
            vm((CBLK,) + blk, BF16),
            vm((zslots,) + blk, F32),
            vm((zslots * pieces, padded, BLK), BF16),
            vm((NG, 2, padded, BLK), BF16),
            vm((2, 8, 128), F32),
            vm((8, 8, 128), F32),
            vm((rest_n, 8, 128), F32),
        ] + [pltpu.SemaphoreType.DMA((n,)) for n in sems],
        compiler_params=pltpu.CompilerParams(
            collective_id=0, has_side_effects=True, vmem_limit_bytes=48 * 1024 * 1024
        ),
    )(acts, cotangents)


def solution(mesh):
    groups, width = mesh.shape["grp"], mesh.shape["dp"]
    spec = P(("grp", "dp"), None)
    return jax.shard_map(
        functools.partial(per_device, groups=groups, width=width),
        mesh=mesh, in_specs=(spec, spec), out_specs=spec, check_vma=False,
    )
```

```python
import functools

import jax
import jax.numpy as jnp
from jax import lax
from jax.experimental import pallas as pl
from jax.experimental.pallas import tpu as pltpu
from jax.sharding import PartitionSpec as P

D = 2560
R = 768
BLK = 128
ITERS = 8
NA = D // BLK
NG = R // BLK
QROWS = D // 4
QBLK = QROWS // BLK
HALF = QROWS // 2
CCOLS = R // 2
CBLK = CCOLS // BLK
SLOTS = 4
MESH = pl.DeviceIdType.MESH
F32 = jnp.float32
BF16 = jnp.bfloat16


def dot(a, b):
    return jnp.dot(a, b, preferred_element_type=F32)


def dot_t(a, b):
    return lax.dot_general(a, b, (((0,), (0,)), ((), ())), preferred_element_type=F32)


def split(a):
    hi = a.astype(BF16)
    return hi, (a - hi.astype(F32)).astype(BF16)


def dot3(a, b):
    ah, al = split(a)
    bh, bl = split(b)
    return dot(jnp.concatenate([ah, ah, al], axis=1), jnp.concatenate([bh, bl, bh], axis=0))


def kernel(
    groups, width, total, rows,
    x_hbm, g_hbm, out_ref,
    x_ref, g_ref, xt, fpart, f1recv, f2send, f2recv, f3send, f3recv,
    m1send, m1recv, macc, m2a, m2s, m2b, mq,
    zsend, zrecv, inv_own, inv_a, inv_g, nat, fin_send, fin_recv, qsend, q1recv, q2recv,
    in_sem,
    f1_ss, f1_rs, f2_ss, f2_rs, f3_ss, f3_rs, m1_ss, m1_rs, ma_ss, ma_rs,
    mb_ss, mb_rs, z_ss, z_rs, inv_ss, inv_rs, fin_ss, fin_rs, q1_ss, q1_rs, q2_ss, q2_rs,
):
    devices = groups * width
    rest_n = devices // 8
    owners = devices // 4
    half_n = devices // 2
    zslots = zsend.shape[1]
    pieces = fin_send.shape[0] // zslots
    dp_rest = width // 4
    gi = lax.axis_index("grp")
    di = lax.axis_index("dp")
    me = gi * width + di
    core = lax.rem(di, 2)
    x = lax.rem(lax.div(di, 2), 2)
    y = lax.rem(gi, 2)
    q = 2 * y + x
    rest = lax.div(gi, 2) * dp_rest + lax.div(di, 4)

    def at(yy, xx, zz, cc):
        return (
            lax.div(zz, dp_rest) * 2 + yy,
            lax.rem(zz, dp_rest) * 4 + xx * 2 + cc,
        )

    def linear(d):
        return (lax.div(d, width), lax.rem(d, width))

    def rcopy(src, dst, ss, rs, dev):
        return pltpu.make_async_remote_copy(
            src_ref=src, dst_ref=dst, send_sem=ss, recv_sem=rs,
            device_id=dev, device_id_type=MESH,
        )

    g_in = pltpu.make_async_copy(g_hbm, g_ref, in_sem.at[4])
    g_in.start()
    x_in = []
    for i in range(4):
        cols = pl.ds(i * QROWS, QROWS)
        x_in.append(pltpu.make_async_copy(x_hbm.at[:, cols], x_ref.at[:, cols], in_sem.at[i]))
        x_in[i].start()

    barrier = pltpu.get_barrier_semaphore()

    def greet(dev):
        pl.semaphore_signal(barrier, inc=1, device_id=dev, device_id_type=MESH)

    greet(at(y, x, rest, 1 - core))
    for yy, xx in ((y, 1 - x), (1 - y, x), (1 - y, 1 - x)):
        greet(at(yy, xx, rest, core))

    @pl.loop(0, rest_n)
    def _(z):
        @pl.when(z != rest)
        def _():
            greet(at(y, x, z, core))

    zero = jnp.zeros((BLK, BLK), BF16)
    g_in.wait()
    for c in range(NG):
        gb = g_ref[:, c * BLK:(c + 1) * BLK]
        fg = dot_t(gb, gb).astype(BF16)
        if c < 4:
            fpart[1, c, 2] = fg
        else:
            fpart[0, c - 4, 3] = fg
    for c in range(4):
        fpart[1, c, 3] = zero
        if c >= NG - 4:
            fpart[0, c, 3] = zero

    for part in range(4):
        x_in[part].wait()
        for b in range(part * QBLK, (part + 1) * QBLK):
            qq, t = b // (2 * QBLK) * 2 + b % 2, b % (2 * QBLK) // 2
            xb = x_ref[:, b * BLK:(b + 1) * BLK]
            xbt = xb.T
            xt[qq * QBLK + t] = xbt
            fpart[t % 2, qq, t // 2] = dot(xbt, xb).astype(BF16)

    pl.semaphore_wait(barrier, rest_n + 3)
    other = at(y, x, rest, 1 - core)
    f1 = rcopy(fpart.at[1 - core], f1recv, f1_ss.at[0], f1_rs.at[0], other)
    f1.start()

    g_other = g_ref[:, pl.ds(pl.multiple_of((1 - core) * CCOLS, BLK), CCOLS)]

    def m1_copy(qq):
        return rcopy(m1send.at[qq], m1recv.at[qq], m1_ss.at[qq], m1_rs.at[qq], other)

    @pl.loop(1, 5)
    def _(turn):
        qq = lax.rem(q + turn, 4)
        for t in range(QBLK):
            m1send[qq, t * BLK:(t + 1) * BLK, :] = dot(xt[qq * QBLK + t], g_other).astype(BF16)
        m1_copy(qq).start()

    f1.wait_recv()

    def f1_sum(qq, s):
        return fpart[core, qq, s].astype(F32) + f1recv[qq, s].astype(F32)

    chips = [(y, 1 - x), (1 - y, x), (1 - y, 1 - x)]
    f2 = []
    for k, (yy, xx) in enumerate(chips):
        qq = 2 * yy + xx
        for s in range(SLOTS):
            f2send[k, s] = f1_sum(qq, s).astype(BF16)
        c2 = rcopy(f2send.at[k], f2recv.at[k], f2_ss.at[k], f2_rs.at[k], at(yy, xx, rest, core))
        c2.start()
        f2.append(c2)

    g_mine = g_ref[:, pl.ds(pl.multiple_of(core * CCOLS, BLK), CCOLS)]

    at_x = at(y, 1 - x, rest, core)
    at_y = at(1 - y, x, rest, core)

    def ma_copy(i, h):
        quarter = 2 * i + (1 - x) if h == 0 else 2 * (1 - y) + i
        k = 2 * h + i
        return rcopy(
            macc.at[quarter, pl.ds(h * HALF, HALF)], m2a.at[k],
            ma_ss.at[k], ma_rs.at[k], at_x if h == 0 else at_y,
        )

    @pl.loop(1, 5)
    def _(turn):
        qq = lax.rem(q + turn, 4)
        m1_copy(qq).wait_recv()
        for t in range(QBLK):
            part = dot(xt[qq * QBLK + t], g_mine)
            sl = slice(t * BLK, (t + 1) * BLK)
            macc[qq, sl, :] = (part + m1recv[qq, sl, :].astype(F32)).astype(BF16)
        yq, xq = lax.div(qq, 2), lax.rem(qq, 2)

        @pl.when(xq != x)
        def _():
            ma_copy(yq, 0).start()

        @pl.when(yq != y)
        def _():
            ma_copy(xq, 1).start()

    ma = [ma_copy(i, h) for i in range(2) for h in range(2)]

    for c2 in f2:
        c2.wait_recv()
    for s in range(SLOTS):
        f = f1_sum(q, s)
        for k in range(3):
            f = f + f2recv[k, s].astype(F32)
        f3send[s] = f.astype(BF16)

    def f3_copy(s, src):
        return rcopy(f3send.at[s], f3recv.at[src], f3_ss.at[s], f3_rs.at[src], at(y, x, s, core))

    for s in range(SLOTS):
        @pl.when(rest != s)
        def _():
            f3_copy(s, rest).start()

    f3recv[rest] = f3send[lax.rem(rest, SLOTS)]

    @pl.when(rest < SLOTS)
    def _():
        @pl.loop(0, rest_n)
        def _(z):
            @pl.when(z != rest)
            def _():
                f3_copy(0, z).wait_recv()

    if rest_n > SLOTS:
        @pl.when(rest >= SLOTS)
        def _():
            @pl.loop(0, rest_n)
            def _(z):
                f3recv[z] = zero

    factor = f3recv[0].astype(F32)
    for z in range(1, rest_n):
        factor = factor + f3recv[z].astype(F32)
    factor = factor * (1.0 / total)

    eye = (
        lax.broadcasted_iota(jnp.int32, (BLK, BLK), 0)
        == lax.broadcasted_iota(jnp.int32, (BLK, BLK), 1)
    ).astype(F32)
    trace = jnp.sum(jnp.sum(factor * eye, axis=1, keepdims=True), axis=0, keepdims=True)
    damped = factor + (0.1 * (trace / BLK + 1e-06)) * eye
    peak = jnp.max(jnp.sum(jnp.abs(damped), axis=1, keepdims=True), axis=0, keepdims=True)
    scale = 1.0 / peak
    approx = scale * (2.0 * eye - scale * damped)
    for _ in range(ITERS - 5):
        approx = dot3(approx, 2.0 * eye - dot3(damped, approx))

    for ca in ma:
        ca.wait_recv()
    for i in range(2):
        for h in range(2):
            k = 2 * h + i
            quarter = 2 * i + x if h == 0 else 2 * y + i
            m2s[k] = (
                macc[quarter, h * HALF:(h + 1) * HALF, :].astype(F32) + m2a[k].astype(F32)
            ).astype(BF16)
    mb = [
        rcopy(m2s.at[1 - y], m2b.at[0], mb_ss.at[0], mb_rs.at[0], at_y),
        rcopy(m2s.at[2 + 1 - x], m2b.at[1], mb_ss.at[1], mb_rs.at[1], at_x),
    ]
    for cb in mb:
        cb.start()

    for _ in range(4):
        approx = dot3(approx, 2.0 * eye - dot3(damped, approx))
    inv_own[...] = approx.astype(BF16)

    slot = 2 * rest + core
    is_a = slot < QBLK
    is_g = jnp.logical_or(slot == QBLK, jnp.logical_and(slot == QBLK + 1, q < NG - 4))
    gidx = (slot - QBLK) * 4 + q
    ghalf = lax.div(gidx, CBLK)

    def a_copy(i, t):
        return rcopy(
            inv_own, inv_a.at[t], inv_ss.at[i], inv_rs.at[t],
            at(y, x, lax.div(i, 2), lax.rem(i, 2)),
        )

    def g_dev(i):
        chip = lax.div(i, rest_n)
        return at(lax.div(chip, 2), lax.rem(chip, 2), lax.rem(i, rest_n), ghalf)

    def g_copy(i, c):
        return rcopy(inv_own, inv_g.at[c], inv_ss.at[i], inv_rs.at[QBLK + c], g_dev(i))

    def not_me(i):
        gg, dd = g_dev(i)
        return gg * width + dd != me

    @pl.when(is_a)
    def _():
        @pl.loop(0, owners)
        def _(i):
            @pl.when(i != slot)
            def _():
                a_copy(i, slot).start()
        inv_a[slot] = inv_own[...]

    @pl.when(is_g)
    def _():
        @pl.loop(0, 4 * rest_n)
        def _(i):
            @pl.when(not_me(i))
            def _():
                g_copy(i, lax.rem(gidx, CBLK)).start()

        @pl.when(ghalf == core)
        def _():
            inv_g[lax.rem(gidx, CBLK)] = inv_own[...]

    for cb in mb:
        cb.wait_recv()
    for h in range(2):
        kept = m2s[y] if h == 0 else m2s[2 + x]
        mq[h * HALF:(h + 1) * HALF, :] = (
            (kept.astype(F32) + m2b[h].astype(F32)) * (1.0 / total)
        ).astype(BF16)

    for i in range(zslots * rest_n):
        t, c = divmod(i, CBLK)
        tile = zero if t >= QBLK else mq[t * BLK:(t + 1) * BLK, c * BLK:(c + 1) * BLK]
        zsend[i // zslots, i % zslots] = tile

    def z_copy(dst, src):
        return rcopy(zsend.at[dst], zrecv.at[src], z_ss.at[dst], z_rs.at[src], at(y, x, dst, core))

    @pl.loop(0, rest_n)
    def _(z):
        @pl.when(z != rest)
        def _():
            z_copy(z, rest).start()

    zrecv[rest] = zsend[rest]

    for c in range(CBLK):
        @pl.when(jnp.logical_not(jnp.logical_and(is_g, gidx == core * CBLK + c)))
        def _():
            g_copy(0, c).wait_recv()
    for t in range(QBLK):
        @pl.when(slot != t)
        def _():
            a_copy(0, t).wait_recv()

    @pl.loop(0, rest_n)
    def _(z):
        @pl.when(z != rest)
        def _():
            z_copy(0, z).wait_recv()

    square = jnp.zeros((1, 1), F32)
    for k in range(zslots):
        tile = rest * zslots + k
        m = zrecv[0, k].astype(F32)
        for z in range(1, rest_n):
            m = m + zrecv[z, k].astype(F32)
        left = dot_t(inv_a[jnp.minimum(lax.div(tile, CBLK), QBLK - 1)], m.astype(BF16))
        hi, lo = split(left)
        ginv = inv_g[lax.rem(tile, CBLK)]
        part = dot(hi, ginv) + dot(lo, ginv)
        nat[k] = part
        square = square + jnp.sum(
            jnp.sum(part * part, axis=0, keepdims=True), axis=1, keepdims=True
        )
    qsend[0] = jnp.broadcast_to(square, (8, 128))

    def q1_copy(p, src):
        return rcopy(
            qsend.at[0], q1recv.at[src], q1_ss.at[p], q1_rs.at[src],
            at(lax.div(p, 4), lax.rem(lax.div(p, 2), 2), rest, lax.rem(p, 2)),
        )

    def q2_copy(z, src):
        return rcopy(qsend.at[1], q2recv.at[src], q2_ss.at[z], q2_rs.at[src], at(y, x, z, core))

    plane = 2 * q + core

    def others(n, mine, body):
        @pl.loop(0, n)
        def _(p):
            @pl.when(p != mine)
            def _():
                body(p)

    others(8, plane, lambda p: q1_copy(p, plane).start())
    q1recv[plane] = qsend[0]

    def each_piece(body):
        for xx in range(2):
            for i in range(QBLK * CBLK):
                t, c = divmod(i, CBLK)
                top = (2 * t + xx) * BLK

                @pl.when(jnp.logical_and(x == xx, rest == i // zslots))
                def _():
                    first = top // rows
                    for k in range(first, (top + BLK + rows - 1) // rows):
                        lo, hi = max(top, k * rows), min(top + BLK, (k + 1) * rows)
                        late = 0 if lo == k * rows else 1
                        body(i % zslots, c, k, lo - k * rows, lo - top, hi - lo, late,
                             i % zslots * pieces + k - first)

    def fin_copy(j, c, late, k):
        return rcopy(
            fin_send.at[j], fin_recv.at[core * CBLK + c, late], fin_ss.at[j],
            fin_rs.at[2 * (core * CBLK + c) + late], linear(y * half_n + k),
        )

    def send_piece(slot_k, c, k, above, start, count, late, j):
        parts = [nat[slot_k, start:start + count, :]]
        if above:
            parts.insert(0, jnp.zeros((above, BLK), F32))
        tail = fin_send.shape[1] - above - count
        if tail:
            parts.append(jnp.zeros((tail, BLK), F32))
        fin_send[j] = (jnp.concatenate(parts, axis=0) if len(parts) > 1 else parts[0]).astype(BF16)

        @pl.when(y * half_n + k != me)
        def _():
            fin_copy(j, c, late, k).start()

        @pl.when(y * half_n + k == me)
        def _():
            fin_recv[core * CBLK + c, late] = fin_send[j]

    each_piece(send_piece)

    others(8, plane, lambda p: q1_copy(0, p).wait_recv())
    qsend[1] = jnp.sum(q1recv[...], axis=0)
    others(rest_n, rest, lambda z: q2_copy(z, rest).start())
    q2recv[rest] = qsend[1]

    k_me = lax.rem(me, half_n)
    t_me = lax.div(k_me * rows, BLK)
    straddles = lax.div(k_me * rows + rows - 1, BLK) > t_me
    mine_here = lax.div(me, half_n) == y
    for late in range(2):
        for c in range(NG):
            from_me = jnp.logical_and(
                jnp.logical_and(mine_here, core == c // CBLK),
                jnp.logical_and(
                    lax.rem(t_me + late, 2) == x,
                    lax.div(CBLK * lax.div(t_me + late, 2) + c % CBLK, zslots) == rest,
                ),
            )
            incoming = jnp.logical_not(from_me)
            if late:
                incoming = jnp.logical_and(straddles, incoming)

                @pl.when(jnp.logical_not(straddles))
                def _():
                    fin_recv[c, 1] = jnp.zeros(fin_recv.shape[2:], BF16)

            @pl.when(incoming)
            def _():
                pltpu.make_async_remote_copy(
                    src_ref=fin_send.at[0], dst_ref=fin_recv.at[c, late], send_sem=fin_ss.at[0],
                    recv_sem=fin_rs.at[2 * c + late], device_id=other, device_id_type=MESH,
                ).wait_recv()

    others(rest_n, rest, lambda z: q2_copy(0, z).wait_recv())
    quad = jnp.sum(q2recv[...], axis=0)[:1, :1] / (D * R)
    factor_out = lax.rsqrt(quad + 1e-06)
    for c in range(NG):
        natural = fin_recv[c, 0].astype(F32) + fin_recv[c, 1].astype(F32)
        out_ref[:, c * BLK:(c + 1) * BLK] = natural[:rows, :] * factor_out

    f1.wait_send()
    for cp in f2 + ma + mb:
        cp.wait_send()

    @pl.loop(0, 4)
    def _(qq):
        m1_copy(qq).wait_send()

    for s in range(SLOTS):
        @pl.when(rest != s)
        def _():
            f3_copy(s, rest).wait_send()

    @pl.when(is_a)
    def _():
        @pl.loop(0, owners)
        def _(i):
            @pl.when(i != slot)
            def _():
                a_copy(i, 0).wait_send()

    @pl.when(is_g)
    def _():
        @pl.loop(0, 4 * rest_n)
        def _(i):
            @pl.when(not_me(i))
            def _():
                g_copy(i, 0).wait_send()

    others(rest_n, rest, lambda z: z_copy(z, 0).wait_send())
    others(8, plane, lambda p: q1_copy(p, 0).wait_send())
    others(rest_n, rest, lambda z: q2_copy(z, 0).wait_send())

    def wait_piece(slot_k, c, k, above, start, count, late, j):
        @pl.when(y * half_n + k != me)
        def _():
            fin_copy(j, c, late, k).wait_send()

    each_piece(wait_piece)


def per_device(acts, cotangents, groups, width):
    tokens = acts.shape[0]
    devices = groups * width
    rest_n = devices // 8
    owners = devices // 4
    rows = D // devices
    padded = (rows + 15) // 16 * 16
    blk = (BLK, BLK)
    zslots = (QBLK * CBLK + rest_n - 1) // rest_n
    pieces = max(
        ((t + 1) * BLK + rows - 1) // rows - t * BLK // rows for t in range(2 * QBLK)
    )
    sems = [5, 1, 1, 3, 3, SLOTS, rest_n, 4, 4, 4, 4, 2, 2, rest_n, rest_n, max(owners, 4 * rest_n),
            QBLK + CBLK, zslots * pieces, 2 * NG, 8, 8, rest_n, rest_n]
    vm = pltpu.VMEM
    return pl.pallas_call(
        functools.partial(kernel, groups, width, tokens * devices, rows),
        out_shape=jax.ShapeDtypeStruct((rows, R), F32),
        in_specs=[pl.BlockSpec(memory_space=pl.ANY)] * 2,
        out_specs=pl.BlockSpec(memory_space=pltpu.VMEM),
        scratch_shapes=[
            vm((tokens, D), BF16),
            vm((tokens, R), BF16),
            vm((NA, BLK, tokens), BF16),
            vm((2, 4, SLOTS) + blk, BF16),
            vm((4, SLOTS) + blk, BF16),
            vm((3, SLOTS) + blk, BF16),
            vm((3, SLOTS) + blk, BF16),
            vm((SLOTS,) + blk, BF16),
            vm((rest_n,) + blk, BF16),
            vm((4, QROWS, CCOLS), BF16),
            vm((4, QROWS, CCOLS), BF16),
            vm((4, QROWS, CCOLS), BF16),
            vm((4, HALF, CCOLS), BF16),
            vm((4, HALF, CCOLS), BF16),
            vm((2, HALF, CCOLS), BF16),
            vm((QROWS, CCOLS), BF16),
            vm((rest_n, zslots) + blk, BF16),
            vm((rest_n, zslots) + blk, BF16),
            vm(blk, BF16),
            vm((QBLK,) + blk, BF16),
            vm((CBLK,) + blk, BF16),
            vm((zslots,) + blk, F32),
            vm((zslots * pieces, padded, BLK), BF16),
            vm((NG, 2, padded, BLK), BF16),
            vm((2, 8, 128), F32),
            vm((8, 8, 128), F32),
            vm((rest_n, 8, 128), F32),
        ] + [pltpu.SemaphoreType.DMA((n,)) for n in sems],
        compiler_params=pltpu.CompilerParams(
            collective_id=0, has_side_effects=True, vmem_limit_bytes=48 * 1024 * 1024
        ),
    )(acts, cotangents)


def solution(mesh):
    groups, width = mesh.shape["grp"], mesh.shape["dp"]
    spec = P(("grp", "dp"), None)
    return jax.shard_map(
        functools.partial(per_device, groups=groups, width=width),
        mesh=mesh, in_specs=(spec, spec), out_specs=spec, check_vma=False,
    )
```

```python
import functools

import jax
import jax.numpy as jnp
from jax import lax
from jax.experimental import pallas as pl
from jax.experimental.pallas import tpu as pltpu
from jax.sharding import PartitionSpec as P

D = 2560
R = 768
BLK = 128
ITERS = 8
NA = D // BLK
NG = R // BLK
QROWS = D // 4
QBLK = QROWS // BLK
HALF = QROWS // 2
CCOLS = R // 2
CBLK = CCOLS // BLK
SLOTS = 4
MESH = pl.DeviceIdType.MESH
F32 = jnp.float32
BF16 = jnp.bfloat16


def dot(a, b):
    return jnp.dot(a, b, preferred_element_type=F32)


def dot_t(a, b):
    return lax.dot_general(a, b, (((0,), (0,)), ((), ())), preferred_element_type=F32)


def split(a):
    hi = a.astype(BF16)
    return hi, (a - hi.astype(F32)).astype(BF16)


def dot3(a, b):
    ah, al = split(a)
    bh, bl = split(b)
    return dot(jnp.concatenate([ah, ah, al], axis=1), jnp.concatenate([bh, bl, bh], axis=0))


def kernel(
    groups, width, total, rows,
    x_hbm, g_hbm, out_ref,
    x_ref, g_ref, xt, fpart, f1recv, f2send, f2recv, f3send, f3recv,
    m1send, m1recv, macc, m2a, m2s, m2b, mq,
    zsend, zrecv, inv_own, inv_a, inv_g, nat, fin_send, fin_recv, qsend, q1recv, q2recv,
    in_sem,
    f1_ss, f1_rs, f2_ss, f2_rs, f3_ss, f3_rs, m1_ss, m1_rs, ma_ss, ma_rs,
    mb_ss, mb_rs, z_ss, z_rs, inv_ss, inv_rs, fin_ss, fin_rs, q1_ss, q1_rs, q2_ss, q2_rs,
):
    devices = groups * width
    rest_n = devices // 8
    owners = devices // 4
    half_n = devices // 2
    zslots = zsend.shape[1]
    pieces = fin_send.shape[0] // zslots
    dp_rest = width // 4
    gi = lax.axis_index("grp")
    di = lax.axis_index("dp")
    me = gi * width + di
    core = lax.rem(di, 2)
    x = lax.rem(lax.div(di, 2), 2)
    y = lax.rem(gi, 2)
    q = 2 * y + x
    rest = lax.div(gi, 2) * dp_rest + lax.div(di, 4)

    def at(yy, xx, zz, cc):
        return (
            lax.div(zz, dp_rest) * 2 + yy,
            lax.rem(zz, dp_rest) * 4 + xx * 2 + cc,
        )

    def linear(d):
        return (lax.div(d, width), lax.rem(d, width))

    def rcopy(src, dst, ss, rs, dev):
        return pltpu.make_async_remote_copy(
            src_ref=src, dst_ref=dst, send_sem=ss, recv_sem=rs,
            device_id=dev, device_id_type=MESH,
        )

    g_in = pltpu.make_async_copy(g_hbm, g_ref, in_sem.at[4])
    g_in.start()
    x_in = []
    for i in range(4):
        cols = pl.ds(i * QROWS, QROWS)
        x_in.append(pltpu.make_async_copy(x_hbm.at[:, cols], x_ref.at[:, cols], in_sem.at[i]))
        x_in[i].start()

    barrier = pltpu.get_barrier_semaphore()

    def greet(dev):
        pl.semaphore_signal(barrier, inc=1, device_id=dev, device_id_type=MESH)

    greet(at(y, x, rest, 1 - core))
    for yy, xx in ((y, 1 - x), (1 - y, x), (1 - y, 1 - x)):
        greet(at(yy, xx, rest, core))

    @pl.loop(0, rest_n)
    def _(z):
        @pl.when(z != rest)
        def _():
            greet(at(y, x, z, core))

    zero = jnp.zeros((BLK, BLK), BF16)
    g_in.wait()
    for c in range(NG):
        gb = g_ref[:, c * BLK:(c + 1) * BLK]
        fg = dot_t(gb, gb).astype(BF16)
        if c < 4:
            fpart[1, c, 2] = fg
        else:
            fpart[0, c - 4, 3] = fg
    for c in range(4):
        fpart[1, c, 3] = zero
        if c >= NG - 4:
            fpart[0, c, 3] = zero

    for part in range(4):
        x_in[part].wait()
        for b in range(part * QBLK, (part + 1) * QBLK):
            qq, t = b // (2 * QBLK) * 2 + b % 2, b % (2 * QBLK) // 2
            xb = x_ref[:, b * BLK:(b + 1) * BLK]
            xbt = xb.T
            xt[qq * QBLK + t] = xbt
            fpart[t % 2, qq, t // 2] = dot(xbt, xb).astype(BF16)

    pl.semaphore_wait(barrier, rest_n + 3)
    other = at(y, x, rest, 1 - core)
    f1 = rcopy(fpart.at[1 - core], f1recv, f1_ss.at[0], f1_rs.at[0], other)
    f1.start()

    g_other = g_ref[:, pl.ds(pl.multiple_of((1 - core) * CCOLS, BLK), CCOLS)]

    def m1_copy(qq):
        return rcopy(m1send.at[qq], m1recv.at[qq], m1_ss.at[qq], m1_rs.at[qq], other)

    @pl.loop(1, 5)
    def _(turn):
        qq = lax.rem(q + turn, 4)
        for t in range(QBLK):
            m1send[qq, t * BLK:(t + 1) * BLK, :] = dot(xt[qq * QBLK + t], g_other).astype(BF16)
        m1_copy(qq).start()

    f1.wait_recv()

    def f1_sum(qq, s):
        return fpart[core, qq, s].astype(F32) + f1recv[qq, s].astype(F32)

    chips = [(y, 1 - x), (1 - y, x), (1 - y, 1 - x)]
    f2 = []
    for k, (yy, xx) in enumerate(chips):
        qq = 2 * yy + xx
        for s in range(SLOTS):
            f2send[k, s] = f1_sum(qq, s).astype(BF16)
        c2 = rcopy(f2send.at[k], f2recv.at[k], f2_ss.at[k], f2_rs.at[k], at(yy, xx, rest, core))
        c2.start()
        f2.append(c2)

    g_mine = g_ref[:, pl.ds(pl.multiple_of(core * CCOLS, BLK), CCOLS)]

    at_x = at(y, 1 - x, rest, core)
    at_y = at(1 - y, x, rest, core)

    def ma_copy(i, h):
        quarter = 2 * i + (1 - x) if h == 0 else 2 * (1 - y) + i
        k = 2 * h + i
        return rcopy(
            macc.at[quarter, pl.ds(h * HALF, HALF)], m2a.at[k],
            ma_ss.at[k], ma_rs.at[k], at_x if h == 0 else at_y,
        )

    @pl.loop(1, 5)
    def _(turn):
        qq = lax.rem(q + turn, 4)
        m1_copy(qq).wait_recv()
        for t in range(QBLK):
            part = dot(xt[qq * QBLK + t], g_mine)
            sl = slice(t * BLK, (t + 1) * BLK)
            macc[qq, sl, :] = (part + m1recv[qq, sl, :].astype(F32)).astype(BF16)
        yq, xq = lax.div(qq, 2), lax.rem(qq, 2)

        @pl.when(xq != x)
        def _():
            ma_copy(yq, 0).start()

        @pl.when(yq != y)
        def _():
            ma_copy(xq, 1).start()

    ma = [ma_copy(i, h) for i in range(2) for h in range(2)]

    for c2 in f2:
        c2.wait_recv()
    for s in range(SLOTS):
        f = f1_sum(q, s)
        for k in range(3):
            f = f + f2recv[k, s].astype(F32)
        f3send[s] = f.astype(BF16)

    def f3_copy(s, src):
        return rcopy(f3send.at[s], f3recv.at[src], f3_ss.at[s], f3_rs.at[src], at(y, x, s, core))

    for s in range(SLOTS):
        @pl.when(rest != s)
        def _():
            f3_copy(s, rest).start()

    f3recv[rest] = f3send[lax.rem(rest, SLOTS)]

    @pl.when(rest < SLOTS)
    def _():
        @pl.loop(0, rest_n)
        def _(z):
            @pl.when(z != rest)
            def _():
                f3_copy(0, z).wait_recv()

    if rest_n > SLOTS:
        @pl.when(rest >= SLOTS)
        def _():
            @pl.loop(0, rest_n)
            def _(z):
                f3recv[z] = zero

    factor = f3recv[0].astype(F32)
    for z in range(1, rest_n):
        factor = factor + f3recv[z].astype(F32)
    factor = factor * (1.0 / total)

    eye = (
        lax.broadcasted_iota(jnp.int32, (BLK, BLK), 0)
        == lax.broadcasted_iota(jnp.int32, (BLK, BLK), 1)
    ).astype(F32)
    trace = jnp.sum(jnp.sum(factor * eye, axis=1, keepdims=True), axis=0, keepdims=True)
    damped = factor + (0.1 * (trace / BLK + 1e-06)) * eye
    peak = jnp.max(jnp.sum(jnp.abs(damped), axis=1, keepdims=True), axis=0, keepdims=True)
    scale = 1.0 / peak
    approx = scale * (2.0 * eye - scale * damped)

    for ca in ma:
        ca.wait_recv()
    for i in range(2):
        for h in range(2):
            k = 2 * h + i
            quarter = 2 * i + x if h == 0 else 2 * y + i
            m2s[k] = (
                macc[quarter, h * HALF:(h + 1) * HALF, :].astype(F32) + m2a[k].astype(F32)
            ).astype(BF16)
    mb = [
        rcopy(m2s.at[1 - y], m2b.at[0], mb_ss.at[0], mb_rs.at[0], at_y),
        rcopy(m2s.at[2 + 1 - x], m2b.at[1], mb_ss.at[1], mb_rs.at[1], at_x),
    ]
    for cb in mb:
        cb.start()

    for _ in range(4):
        approx = dot3(approx, 2.0 * eye - dot3(damped, approx))
    for cb in mb:
        cb.wait_recv()
    for h in range(2):
        kept = m2s[y] if h == 0 else m2s[2 + x]
        mq[h * HALF:(h + 1) * HALF, :] = (
            (kept.astype(F32) + m2b[h].astype(F32)) * (1.0 / total)
        ).astype(BF16)

    for i in range(zslots * rest_n):
        t, c = divmod(i, CBLK)
        tile = zero if t >= QBLK else mq[t * BLK:(t + 1) * BLK, c * BLK:(c + 1) * BLK]
        zsend[i // zslots, i % zslots] = tile

    def z_copy(dst, src):
        return rcopy(zsend.at[dst], zrecv.at[src], z_ss.at[dst], z_rs.at[src], at(y, x, dst, core))

    @pl.loop(0, rest_n)
    def _(z):
        @pl.when(z != rest)
        def _():
            z_copy(z, rest).start()

    zrecv[rest] = zsend[rest]

    for _ in range(ITERS - 5):
        approx = dot3(approx, 2.0 * eye - dot3(damped, approx))
    inv_own[...] = approx.astype(BF16)

    slot = 2 * rest + core
    is_a = slot < QBLK
    is_g = jnp.logical_or(slot == QBLK, jnp.logical_and(slot == QBLK + 1, q < NG - 4))
    gidx = (slot - QBLK) * 4 + q
    ghalf = lax.div(gidx, CBLK)

    def a_copy(i, t):
        return rcopy(
            inv_own, inv_a.at[t], inv_ss.at[i], inv_rs.at[t],
            at(y, x, lax.div(i, 2), lax.rem(i, 2)),
        )

    def g_dev(i):
        chip = lax.div(i, rest_n)
        return at(lax.div(chip, 2), lax.rem(chip, 2), lax.rem(i, rest_n), ghalf)

    def g_copy(i, c):
        return rcopy(inv_own, inv_g.at[c], inv_ss.at[i], inv_rs.at[QBLK + c], g_dev(i))

    def not_me(i):
        gg, dd = g_dev(i)
        return gg * width + dd != me

    @pl.when(is_a)
    def _():
        @pl.loop(0, owners)
        def _(i):
            @pl.when(i != slot)
            def _():
                a_copy(i, slot).start()
        inv_a[slot] = inv_own[...]

    @pl.when(is_g)
    def _():
        @pl.loop(0, 4 * rest_n)
        def _(i):
            @pl.when(not_me(i))
            def _():
                g_copy(i, lax.rem(gidx, CBLK)).start()

        @pl.when(ghalf == core)
        def _():
            inv_g[lax.rem(gidx, CBLK)] = inv_own[...]

    for c in range(CBLK):
        @pl.when(jnp.logical_not(jnp.logical_and(is_g, gidx == core * CBLK + c)))
        def _():
            g_copy(0, c).wait_recv()
    for t in range(QBLK):
        @pl.when(slot != t)
        def _():
            a_copy(0, t).wait_recv()

    @pl.loop(0, rest_n)
    def _(z):
        @pl.when(z != rest)
        def _():
            z_copy(0, z).wait_recv()

    square = jnp.zeros((1, 1), F32)
    for k in range(zslots):
        tile = rest * zslots + k
        m = zrecv[0, k].astype(F32)
        for z in range(1, rest_n):
            m = m + zrecv[z, k].astype(F32)
        left = dot_t(inv_a[jnp.minimum(lax.div(tile, CBLK), QBLK - 1)], m.astype(BF16))
        hi, lo = split(left)
        ginv = inv_g[lax.rem(tile, CBLK)]
        part = dot(hi, ginv) + dot(lo, ginv)
        nat[k] = part
        square = square + jnp.sum(
            jnp.sum(part * part, axis=0, keepdims=True), axis=1, keepdims=True
        )
    qsend[0] = jnp.broadcast_to(square, (8, 128))

    def q1_copy(p, src):
        return rcopy(
            qsend.at[0], q1recv.at[src], q1_ss.at[p], q1_rs.at[src],
            at(lax.div(p, 4), lax.rem(lax.div(p, 2), 2), rest, lax.rem(p, 2)),
        )

    def q2_copy(z, src):
        return rcopy(qsend.at[1], q2recv.at[src], q2_ss.at[z], q2_rs.at[src], at(y, x, z, core))

    plane = 2 * q + core

    def others(n, mine, body):
        @pl.loop(0, n)
        def _(p):
            @pl.when(p != mine)
            def _():
                body(p)

    others(8, plane, lambda p: q1_copy(p, plane).start())
    q1recv[plane] = qsend[0]

    def each_piece(body):
        for xx in range(2):
            for i in range(QBLK * CBLK):
                t, c = divmod(i, CBLK)
                top = (2 * t + xx) * BLK

                @pl.when(jnp.logical_and(x == xx, rest == i // zslots))
                def _():
                    first = top // rows
                    for k in range(first, (top + BLK + rows - 1) // rows):
                        lo, hi = max(top, k * rows), min(top + BLK, (k + 1) * rows)
                        late = 0 if lo == k * rows else 1
                        body(i % zslots, c, k, lo - k * rows, lo - top, hi - lo, late,
                             i % zslots * pieces + k - first)

    def fin_copy(j, c, late, k):
        return rcopy(
            fin_send.at[j], fin_recv.at[core * CBLK + c, late], fin_ss.at[j],
            fin_rs.at[2 * (core * CBLK + c) + late], linear(y * half_n + k),
        )

    def send_piece(slot_k, c, k, above, start, count, late, j):
        parts = [nat[slot_k, start:start + count, :]]
        if above:
            parts.insert(0, jnp.zeros((above, BLK), F32))
        tail = fin_send.shape[1] - above - count
        if tail:
            parts.append(jnp.zeros((tail, BLK), F32))
        fin_send[j] = (jnp.concatenate(parts, axis=0) if len(parts) > 1 else parts[0]).astype(BF16)

        @pl.when(y * half_n + k != me)
        def _():
            fin_copy(j, c, late, k).start()

        @pl.when(y * half_n + k == me)
        def _():
            fin_recv[core * CBLK + c, late] = fin_send[j]

    each_piece(send_piece)

    others(8, plane, lambda p: q1_copy(0, p).wait_recv())
    qsend[1] = jnp.sum(q1recv[...], axis=0)
    others(rest_n, rest, lambda z: q2_copy(z, rest).start())
    q2recv[rest] = qsend[1]

    k_me = lax.rem(me, half_n)
    t_me = lax.div(k_me * rows, BLK)
    straddles = lax.div(k_me * rows + rows - 1, BLK) > t_me
    mine_here = lax.div(me, half_n) == y
    for late in range(2):
        for c in range(NG):
            from_me = jnp.logical_and(
                jnp.logical_and(mine_here, core == c // CBLK),
                jnp.logical_and(
                    lax.rem(t_me + late, 2) == x,
                    lax.div(CBLK * lax.div(t_me + late, 2) + c % CBLK, zslots) == rest,
                ),
            )
            incoming = jnp.logical_not(from_me)
            if late:
                incoming = jnp.logical_and(straddles, incoming)

                @pl.when(jnp.logical_not(straddles))
                def _():
                    fin_recv[c, 1] = jnp.zeros(fin_recv.shape[2:], BF16)

            @pl.when(incoming)
            def _():
                pltpu.make_async_remote_copy(
                    src_ref=fin_send.at[0], dst_ref=fin_recv.at[c, late], send_sem=fin_ss.at[0],
                    recv_sem=fin_rs.at[2 * c + late], device_id=other, device_id_type=MESH,
                ).wait_recv()

    others(rest_n, rest, lambda z: q2_copy(0, z).wait_recv())
    quad = jnp.sum(q2recv[...], axis=0)[:1, :1] / (D * R)
    factor_out = lax.rsqrt(quad + 1e-06)
    for c in range(NG):
        natural = fin_recv[c, 0].astype(F32) + fin_recv[c, 1].astype(F32)
        out_ref[:, c * BLK:(c + 1) * BLK] = natural[:rows, :] * factor_out

    f1.wait_send()
    for cp in f2 + ma + mb:
        cp.wait_send()

    @pl.loop(0, 4)
    def _(qq):
        m1_copy(qq).wait_send()

    for s in range(SLOTS):
        @pl.when(rest != s)
        def _():
            f3_copy(s, rest).wait_send()

    @pl.when(is_a)
    def _():
        @pl.loop(0, owners)
        def _(i):
            @pl.when(i != slot)
            def _():
                a_copy(i, 0).wait_send()

    @pl.when(is_g)
    def _():
        @pl.loop(0, 4 * rest_n)
        def _(i):
            @pl.when(not_me(i))
            def _():
                g_copy(i, 0).wait_send()

    others(rest_n, rest, lambda z: z_copy(z, 0).wait_send())
    others(8, plane, lambda p: q1_copy(p, 0).wait_send())
    others(rest_n, rest, lambda z: q2_copy(z, 0).wait_send())

    def wait_piece(slot_k, c, k, above, start, count, late, j):
        @pl.when(y * half_n + k != me)
        def _():
            fin_copy(j, c, late, k).wait_send()

    each_piece(wait_piece)


def per_device(acts, cotangents, groups, width):
    tokens = acts.shape[0]
    devices = groups * width
    rest_n = devices // 8
    owners = devices // 4
    rows = D // devices
    padded = (rows + 15) // 16 * 16
    blk = (BLK, BLK)
    zslots = (QBLK * CBLK + rest_n - 1) // rest_n
    pieces = max(
        ((t + 1) * BLK + rows - 1) // rows - t * BLK // rows for t in range(2 * QBLK)
    )
    sems = [5, 1, 1, 3, 3, SLOTS, rest_n, 4, 4, 4, 4, 2, 2, rest_n, rest_n, max(owners, 4 * rest_n),
            QBLK + CBLK, zslots * pieces, 2 * NG, 8, 8, rest_n, rest_n]
    vm = pltpu.VMEM
    return pl.pallas_call(
        functools.partial(kernel, groups, width, tokens * devices, rows),
        out_shape=jax.ShapeDtypeStruct((rows, R), F32),
        in_specs=[pl.BlockSpec(memory_space=pl.ANY)] * 2,
        out_specs=pl.BlockSpec(memory_space=pltpu.VMEM),
        scratch_shapes=[
            vm((tokens, D), BF16),
            vm((tokens, R), BF16),
            vm((NA, BLK, tokens), BF16),
            vm((2, 4, SLOTS) + blk, BF16),
            vm((4, SLOTS) + blk, BF16),
            vm((3, SLOTS) + blk, BF16),
            vm((3, SLOTS) + blk, BF16),
            vm((SLOTS,) + blk, BF16),
            vm((rest_n,) + blk, BF16),
            vm((4, QROWS, CCOLS), BF16),
            vm((4, QROWS, CCOLS), BF16),
            vm((4, QROWS, CCOLS), BF16),
            vm((4, HALF, CCOLS), BF16),
            vm((4, HALF, CCOLS), BF16),
            vm((2, HALF, CCOLS), BF16),
            vm((QROWS, CCOLS), BF16),
            vm((rest_n, zslots) + blk, BF16),
            vm((rest_n, zslots) + blk, BF16),
            vm(blk, BF16),
            vm((QBLK,) + blk, BF16),
            vm((CBLK,) + blk, BF16),
            vm((zslots,) + blk, F32),
            vm((zslots * pieces, padded, BLK), BF16),
            vm((NG, 2, padded, BLK), BF16),
            vm((2, 8, 128), F32),
            vm((8, 8, 128), F32),
            vm((rest_n, 8, 128), F32),
        ] + [pltpu.SemaphoreType.DMA((n,)) for n in sems],
        compiler_params=pltpu.CompilerParams(
            collective_id=0, has_side_effects=True, vmem_limit_bytes=48 * 1024 * 1024
        ),
    )(acts, cotangents)


def solution(mesh):
    groups, width = mesh.shape["grp"], mesh.shape["dp"]
    spec = P(("grp", "dp"), None)
    return jax.shard_map(
        functools.partial(per_device, groups=groups, width=width),
        mesh=mesh, in_specs=(spec, spec), out_specs=spec, check_vma=False,
    )
```
